512 devices in a mesh: dp: 16 (over z_hi, y), tile: 32 (over z_lo, x, core).
Axes of the slice: x: 4, y: 8, z: 8 (z_hi: 2, z_lo: 4; z = z_hi * 4 + z_lo), core: 2. Of those that a mesh axis runs over, the one named last changes fastest.
Arguments:
- activations: bfloat16 [3072, 53248], P('dp', 'tile'), may hold values from -6 to 6
- sign_bits: int32 [53248], P('tile'), may hold values from 0 to 1
- factor_bits: int32 [13], replicated, may hold values from 0 to 1
Outputs:
- gram_slab: float32 [256, 53248], P('dp', 'tile')
The draws below stay inside these ranges and needn't reach their ends.
All inputs are finite; a program needn't handle non-finite values.
Results may differ from the reference program's by a relative error of at most 0.0083.
Values may be sent and summed in bfloat16 or wider, within the bound.
A program may use at most 128 MiB of HBM per device.

```python
import jax
import jax.numpy as jnp
from jax import lax

D = 53248
KF = 13
HB = 128
TS = 128
TOK_DEV = 192
SLAB = 256
HAD = 4096
TOKENS = 3072
N_DP = 16


def plant(drawn, own_key, low, high):
    longest = drawn.shape.index(max(drawn.shape))
    spots = []
    for shift in (0, 1):
        where = [jax.random.randint(jax.random.fold_in(own_key, axis), (), 0, length) for axis, length in enumerate(drawn.shape)]
        where[longest] = (where[longest] + shift) % drawn.shape[longest]
        spots.append(tuple(where))
    return drawn.at[spots[0]].set(low).at[spots[1]].set(high)


def block_scale(own_key, dims, shards, low, top_value):
    loudness, own = 1.0, jax.random.fold_in(own_key, 6)
    for dim, shards_of in shards:
        steps = jnp.exp(jax.random.uniform(jax.random.fold_in(own, dim), (shards_of,), jnp.float32, low / len(shards), top_value / len(shards)))
        loudness = loudness * jnp.repeat(steps, dims[dim] // shards_of).reshape([-1 if axis == dim else 1 for axis in range(len(dims))])
    return loudness


def noise(stream_key, dims, scale, most, split=(), kind=jnp.bfloat16):
    gain = block_scale(stream_key, dims, split, -0.22, 0.18) if split else 1.0
    entries = jax.random.normal(stream_key, dims, jnp.float32) * scale * gain
    return jnp.minimum(jnp.maximum(entries, -most), most).astype(kind)


def setup_inputs(seed: int = 0) -> dict:
    splits = jax.random.split(jax.random.key(seed), 4)
    return {
        "activations": noise(splits[0], (TOKENS, D), 1.0, 6.0, ((0, 16), (1, 32))),
        "sign_bits": plant(jax.random.randint(splits[1], (D,), 0, 2), jax.random.fold_in(splits[1], 1), 0, 1).astype(jnp.int32),
        "factor_bits": plant(jax.random.randint(splits[2], (KF,), 0, 2), jax.random.fold_in(splits[2], 1), 0, 1).astype(jnp.int32),
    }


def sylvester(order):
    index = jnp.arange(order, dtype=jnp.int32)
    both = index[:, None] & index[None, :]
    parity = jnp.zeros((order, order), jnp.int32)
    for shift in range(order.bit_length() - 1):
        parity = parity ^ both >> shift & 1
    return (1 - 2 * parity).astype(jnp.float32)

def reference(activations, sign_bits, factor_bits):
    width = HB * KF
    groups = D // width
    flipped = activations * (1 - 2 * sign_bits).astype(jnp.bfloat16)[None, :]
    vector = (1 - 2 * factor_bits).astype(jnp.float32)
    reflect = jnp.eye(KF, dtype=jnp.float32) - 2.0 / KF * vector[:, None] * vector[None, :]
    hblock = sylvester(HB)
    factor = (hblock[:, None, :, None] * reflect[None, :, None, :]).reshape(width, width).astype(jnp.bfloat16)
    hgroup = sylvester(groups)
    scale = 1.0 / math_sqrt(HAD)
    blocks = flipped.reshape(N_DP, TOK_DEV, D)

    def one_block(total, rows):
        inner = jnp.dot(rows.reshape(TOK_DEV * groups, width), factor, preferred_element_type=jnp.float32)
        inner = inner.reshape(TOK_DEV, groups, width)
        mixed = jnp.einsum('kl,tlc->tkc', hgroup, inner, precision=lax.Precision.HIGHEST)
        rotated = (mixed * scale).reshape(TOK_DEV, D).astype(jnp.bfloat16)
        slab = rotated[:, :SLAB]
        term = jnp.einsum('tr,tc->rc', slab, rotated, preferred_element_type=jnp.float32)
        return (total + term, None)
    total, _ = lax.scan(one_block, jnp.zeros((SLAB, D), jnp.float32), blocks)
    row_tile = jnp.arange(SLAB, dtype=jnp.int32) // TS
    col_tile = jnp.arange(D, dtype=jnp.int32) // TS
    keep = col_tile[None, :] >= row_tile[:, None]
    return jnp.where(keep, total * (2.0 / TOKENS), 0.0)

def math_sqrt(value):
    return float(value) ** 0.5
```

```python
import functools

import jax
import jax.numpy as jnp
import ml_dtypes
import numpy as np
from jax import lax
from jax.experimental import pallas as pl
from jax.experimental.pallas import tpu as pltpu
from jax.sharding import PartitionSpec as P

KF = 13
HB = 128
WIDTH = KF * HB
SLAB = 256
HAD = 4096
LANES = 128
NT = WIDTH // LANES
MESH = pl.DeviceIdType.MESH
BF = jnp.bfloat16
F32 = jnp.float32


def small_factor():
    index = np.arange(HB)
    both = index[:, None] & index[None, :]
    parity = np.zeros_like(both)
    for shift in range(7):
        parity ^= (both >> shift) & 1
    hblock = (1 - 2 * parity).astype(np.float32)
    refl = np.eye(KF, dtype=np.float32) - np.float32(2.0 / KF)
    return np.kron(hblock, refl).astype(ml_dtypes.bfloat16)


def butterfly(parts):
    step = 1
    parts = list(parts)
    while step < len(parts):
        for low in range(len(parts)):
            if not low & step:
                a, b = parts[low], parts[low | step]
                parts[low], parts[low | step] = a + b, a - b
        step *= 2
    return parts


def parity_sign(mine, other, bits):
    total = 0
    for bit in range(bits):
        if other >> bit & 1:
            total = total + mine // (1 << bit) % 2
    return (1 - 2 * (total % 2)).astype(F32) if not isinstance(total, int) else None


def kernel(
    dims,
    act_hbm, sign_ref, bits_ref, fac_hbm,
    out_ref,
    x_buf, fac_buf, inner, ysend, yrecv, ymid, yzrecv, yfull,
    gp, rs, pbuf, zbuf, zlast, ubuf, xbuf, wbuf, obuf,
    load_sem, y1s, y1r, y2s, y2r, y3s, y3r, rss, rsr, zs, zr, xs_s, xs_r, as_s, as_r,
):
    ny, nzl, nx, nc = dims
    nxc = nx * nc
    rows = SLAB // (2 * ny)
    tokens = act_hbm.shape[0]
    piece = tokens // nx
    nch = NT // nzl
    dp, tile = lax.axis_index("dp"), lax.axis_index("tile")
    zh, y = dp // ny, dp % ny
    zl, xc = tile // nxc, tile % nxc

    def at(zh_, y_, zl_, xc_):
        return (zh_ * ny + y_, zl_ * nxc + xc_)

    def xc_peer(k):
        return at(zh, y, zl, (xc + k) % nxc)

    def z_peer(a, k):
        return at((zh + a) % 2, y, (zl + k) % nzl, xc)

    z_moves = [(a, k) for a in range(2) for k in range(nzl) if (a, k) != (0, 0)]

    def remote(src, dst, send, recv, peer):
        copy = pltpu.make_async_remote_copy(
            src_ref=src, dst_ref=dst, send_sem=send, recv_sem=recv, device_id=peer, device_id_type=MESH
        )
        copy.start()
        return copy

    load_x = pltpu.make_async_copy(act_hbm, x_buf, load_sem.at[0])
    load_a = pltpu.make_async_copy(fac_hbm.at[:, pl.ds(0, SLAB)], fac_buf.at[:, pl.ds(0, SLAB)], load_sem.at[1])
    load_b = pltpu.make_async_copy(
        fac_hbm.at[:, pl.ds(SLAB, WIDTH - SLAB)], fac_buf.at[:, pl.ds(SLAB, WIDTH - SLAB)], load_sem.at[2]
    )
    load_x.start()
    load_a.start()
    load_b.start()

    barrier = pltpu.get_barrier_semaphore()
    peers = [xc_peer(k) for k in range(1, nxc)] + [z_peer(a, k) for a, k in z_moves]
    peers += [at(zh, (y + 1) % ny, zl, xc), at(zh, (y + ny - 1) % ny, zl, xc)]
    for peer in peers:
        pl.semaphore_signal(barrier, inc=1, device_id=peer, device_id_type=MESH)

    col = lax.broadcasted_iota(jnp.int32, (1, WIDTH), 1)
    b_of = col - KF * ((col * 20165) >> 18)
    vee = jnp.zeros((1, WIDTH), F32)
    for b in range(KF):
        vee = jnp.where(b_of == b, (1 - 2 * bits_ref[b]).astype(F32), vee)
    flip = ((1 - 2 * sign_ref[...]).astype(F32) * vee).astype(BF)

    load_x.wait()
    x_buf[...] = x_buf[...] * flip
    load_a.wait()

    part = jnp.dot(x_buf[...], fac_buf[:, :SLAB], preferred_element_type=F32) * vee[:, :SLAB]
    inner[:, :SLAB] = part.astype(BF)
    for ix in range(nx):
        for ic in range(2):
            ysend[ix * 2 + ic] = part[ix * piece:(ix + 1) * piece, ic * LANES:(ic + 1) * LANES].astype(BF)
    pl.semaphore_wait(barrier, len(peers))

    def more_inner(first, last):
        for c0 in range(first, last, 256):
            c1 = min(c0 + 256, last)
            got = jnp.dot(x_buf[...], fac_buf[:, c0:c1], preferred_element_type=F32) * vee[:, c0:c1]
            inner[:, c0:c1] = got.astype(BF)

    moves = [
        remote(ysend.at[(xc + k) % nxc], yrecv.at[k], y1s.at[k], y1r.at[k], xc_peer(k)) for k in range(1, nxc)
    ]
    load_b.wait()
    more_inner(256, 768)
    total = ysend[xc].astype(F32)
    for k in range(1, nxc):
        moves[k - 1].wait_recv()
        total = total + yrecv[k].astype(F32)
    ymid[...] = total.astype(BF)
    moves2 = [
        remote(ymid, yzrecv.at[k], y2s.at[k], y2r.at[k], z_peer(0, k)) for k in range(1, nzl)
    ]
    more_inner(768, 1280)
    total = ymid[...].astype(F32)
    for k in range(1, nzl):
        moves2[k - 1].wait_recv()
        total = total + yzrecv[k].astype(F32)
    yfull[xc] = total.astype(BF)
    moves3 = [
        remote(yfull.at[xc], yfull.at[xc], y3s.at[k], y3r.at[k], xc_peer(k)) for k in range(1, nxc)
    ]
    more_inner(1280, WIDTH)
    for move in moves3:
        move.wait_recv()

    for half in range(2):
        left = jnp.concatenate([yfull[ix * 2 + half] for ix in range(nx)], axis=0)
        for c0 in range(0, WIDTH, 256):
            c1 = min(c0 + 256, WIDTH)
            got = lax.dot_general(
                left, inner[:, c0:c1], (((0,), (0,)), ((), ())), preferred_element_type=F32
            ).astype(BF)
            for iy in range(ny):
                for j in range((c1 - c0) // LANES):
                    gp[iy, half, c0 // LANES + j] = got[iy * rows:(iy + 1) * rows, j * LANES:(j + 1) * LANES]

    chunks = [(nzl * m, nzl * m + nzl if m < nch - 1 else NT) for m in range(nch)]
    top = ny // 2
    ways = [(way, half) for way in range(2) for half in range(2)]
    rs_moves = {}

    def far(way, half):
        return top if way == half else top - 1

    def rs_send(src, way, half, dist, m):
        lo, hi = chunks[m]
        step = 1 if way == 0 else ny - 1
        index = ((way * 2 + half) * top + dist - 1) * nch + m
        rs_moves[way, half, dist, m] = remote(
            src, rs.at[way, half, dist - 1, pl.ds(lo, hi - lo)], rss.at[index], rsr.at[index],
            at(zh, (y + step) % ny, zl, xc),
        )

    def owner(way, dist):
        return (y + dist) % ny if way == 0 else (y + ny - dist) % ny

    for m in range(nch):
        lo, hi = chunks[m]
        for way, half in ways:
            dist = far(way, half)
            if dist == top:
                rs_send(gp.at[owner(way, dist), half, pl.ds(lo, hi - lo)], way, half, dist, m)
        for way, half in ways:
            dist = far(way, half)
            if 0 < dist < top:
                rs_send(gp.at[owner(way, dist), half, pl.ds(lo, hi - lo)], way, half, dist, m)
    for dist in range(top - 1, 0, -1):
        for m in range(nch):
            lo, hi = chunks[m]
            for way, half in ways:
                if dist < far(way, half):
                    rs_moves[way, half, dist + 1, m].wait_recv()
                    slot = rs.at[way, half, dist, pl.ds(lo, hi - lo)]
                    slot[...] = (
                        slot[...].astype(F32) + gp[owner(way, dist), half, pl.ds(lo, hi - lo)].astype(F32)
                    ).astype(BF)
                    rs_send(slot, way, half, dist, m)

    z_copies, x_copies, a_copies = {}, {}, {}
    for m in range(nch):
        lo, hi = chunks[m]
        for half in range(2):
            total = gp[y, half, pl.ds(lo, hi - lo)].astype(F32)
            for way in range(2):
                if (way, half, 1, m) in rs_moves:
                    rs_moves[way, half, 1, m].wait_recv()
                    total = total + rs[way, half, 0, pl.ds(lo, hi - lo)].astype(F32)
            pbuf[half, pl.ds(lo, hi - lo)] = total.astype(BF)
        for n, (a, k) in enumerate(z_moves):
            index = m * len(z_moves) + n
            z_copies[m, n] = remote(
                pbuf.at[(zh + a) % 2, lo + (zl + k) % nzl], zbuf.at[m, zh, zl], zs.at[index], zr.at[index], z_peer(a, k)
            )
        zbuf[m, zh, zl] = pbuf[zh, lo + zl]
        if hi - lo > nzl:
            for n, (a, k) in enumerate(z_moves):
                index = nch * len(z_moves) + n
                z_copies[nch, n] = remote(
                    pbuf.at[(zh + a) % 2, NT - 1], zlast.at[zh, zl], zs.at[index], zr.at[index], z_peer(a, k)
                )
            zlast[zh, zl] = pbuf[zh, NT - 1]

    zbits = nzl.bit_length() - 1
    xbits = nxc.bit_length() - 1

    def mix(parts, mine, bits):
        total = None
        for j, value in enumerate(parts):
            sign = parity_sign(mine, j, bits)
            value = value if sign is None else value * sign
            total = value if total is None else total + value
        return total

    for m in range(nch):
        lo, hi = chunks[m]
        count = hi - lo
        for n in range(len(z_moves)):
            z_copies[m, n].wait_recv()
        mixed = butterfly([zbuf[m, 0, l].astype(F32) + zbuf[m, 1, l].astype(F32) for l in range(nzl)])
        for kz in range(nzl):
            ubuf[lo + kz] = mixed[kz].astype(BF)
        if count > nzl:
            for n in range(len(z_moves)):
                z_copies[nch, n].wait_recv()
            ubuf[NT - 1] = mix(
                [zlast[0, l].astype(F32) + zlast[1, l].astype(F32) for l in range(nzl)], zl, zbits
            ).astype(BF)
        for k in range(1, nxc):
            index = m * nxc + k
            x_copies[m, k] = remote(
                ubuf.at[pl.ds(lo, count)], xbuf.at[xc, pl.ds(lo, count)], xs_s.at[index], xs_r.at[index], xc_peer(k)
            )
        xbuf[xc, pl.ds(lo, count)] = ubuf[pl.ds(lo, count)]

    for m in range(nch):
        lo, hi = chunks[m]
        count = hi - lo
        for k in range(1, nxc):
            x_copies[m, k].wait_recv()
        full = mix([xbuf[j, pl.ds(lo, count)].astype(F32) for j in range(nxc)], xc, xbits)
        wbuf[pl.ds(lo, count)] = full.astype(BF)
        for k in range(1, nzl):
            index = m * nzl + k
            a_copies[m, k] = remote(
                wbuf.at[lo + (zl + k) % nzl], obuf.at[lo + zl], as_s.at[index], as_r.at[index], z_peer(0, k)
            )
        obuf[lo + zl] = wbuf[lo + zl]
        if count > nzl:
            out_ref[:, (NT - 1) * LANES:] = full[count - 1]

    for m in range(nch):
        lo, hi = chunks[m]
        for k in range(1, nzl):
            a_copies[m, k].wait_recv()
        for j in range(nzl):
            out_ref[:, (lo + j) * LANES:(lo + j + 1) * LANES] = obuf[lo + j].astype(F32)

    for group in (moves, moves2, moves3, rs_moves.values(), z_copies.values(), x_copies.values(), a_copies.values()):
        for move in group:
            move.wait_send()


def shards(dims, activations, sign_bits, factor_bits):
    ny, nzl, nx, nc = dims
    nxc = nx * nc
    rows = SLAB // (2 * ny)
    tokens = activations.shape[0]
    piece = tokens // nx
    nch = NT // nzl
    top = ny // 2
    dma = pltpu.SemaphoreType.DMA
    vm = pltpu.VMEM
    n_rs = 4 * top * nch
    n_z = (nch + 1) * (2 * nzl - 1)
    n_x = nch * nxc
    n_a = nch * nzl
    gram = pl.pallas_call(
        functools.partial(kernel, dims),
        out_shape=jax.ShapeDtypeStruct((rows, WIDTH), F32),
        in_specs=[
            pl.BlockSpec(memory_space=pl.ANY),
            pl.BlockSpec(memory_space=pltpu.VMEM),
            pl.BlockSpec(memory_space=pltpu.SMEM),
            pl.BlockSpec(memory_space=pl.ANY),
        ],
        out_specs=pl.BlockSpec(memory_space=pltpu.VMEM),
        scratch_shapes=[
            vm((tokens, WIDTH), BF),
            vm((WIDTH, WIDTH), BF),
            vm((tokens, WIDTH), BF),
            vm((nxc, piece, LANES), BF),
            vm((nxc, piece, LANES), BF),
            vm((piece, LANES), BF),
            vm((nzl, piece, LANES), BF),
            vm((nxc, piece, LANES), BF),
            vm((ny, 2, NT, rows, LANES), BF),
            vm((2, 2, top, NT, rows, LANES), BF),
            vm((2, NT, rows, LANES), BF),
            vm((nch, 2, nzl, rows, LANES), BF),
            vm((2, nzl, rows, LANES), BF),
            vm((NT, rows, LANES), BF),
            vm((nxc, NT, rows, LANES), BF),
            vm((NT, rows, LANES), BF),
            vm((NT, rows, LANES), BF),
            dma((3,)),
            dma((nxc,)), dma((nxc,)),
            dma((nzl,)), dma((nzl,)),
            dma((nxc,)), dma((nxc,)),
            dma((n_rs,)), dma((n_rs,)),
            dma((n_z,)), dma((n_z,)),
            dma((n_x,)), dma((n_x,)),
            dma((n_a,)), dma((n_a,)),
        ],
        compiler_params=pltpu.CompilerParams(
            collective_id=0, has_side_effects=True, vmem_limit_bytes=40 * 1024 * 1024
        ),
    )(activations, sign_bits.reshape(1, WIDTH), factor_bits, jnp.asarray(small_factor()))
    row = lax.axis_index("dp") * rows + lax.broadcasted_iota(jnp.int32, gram.shape, 0)
    col = lax.axis_index("tile") * WIDTH + lax.broadcasted_iota(jnp.int32, gram.shape, 1)
    keep = col // LANES >= row // LANES
    all_tokens = tokens * 2 * ny
    return jnp.where(keep, gram * (2.0 / all_tokens / HAD), 0.0)


def solution(mesh, dims=(8, 4, 4, 2)):
    return jax.shard_map(
        functools.partial(shards, dims),
        mesh=mesh,
        in_specs=(P("dp", "tile"), P("tile"), P()),
        out_specs=P("dp", "tile"),
        check_vma=False,
    )
```

```python
import functools

import jax
import jax.numpy as jnp
import ml_dtypes
import numpy as np
from jax import lax
from jax.experimental import pallas as pl
from jax.experimental.pallas import tpu as pltpu
from jax.sharding import PartitionSpec as P

KF = 13
HB = 128
WIDTH = KF * HB
SLAB = 256
HAD = 4096
LANES = 128
NT = WIDTH // LANES
CHUNKS = 3
VMEM_LIMIT = 60 * 1024 * 1024
MESH = pl.DeviceIdType.MESH
BF = jnp.bfloat16
F32 = jnp.float32


def small_factor():
    index = np.arange(HB)
    both = index[:, None] & index[None, :]
    parity = np.zeros_like(both)
    for shift in range(7):
        parity ^= (both >> shift) & 1
    hblock = (1 - 2 * parity).astype(np.float32)
    refl = np.eye(KF, dtype=np.float32) - np.float32(2.0 / KF)
    return np.kron(hblock, refl).astype(ml_dtypes.bfloat16)


def butterfly(parts):
    step = 1
    parts = list(parts)
    while step < len(parts):
        for low in range(len(parts)):
            if not low & step:
                a, b = parts[low], parts[low | step]
                parts[low], parts[low | step] = a + b, a - b
        step *= 2
    return parts


def kernel(
    dims,
    act_hbm, sign_ref, bits_hbm, fac_hbm,
    out_ref,
    x_buf, fac_buf, inner, other, bits_ref, ysend, yrecv, ymid, yzrecv, yfull,
    gp, rs_agg, rs_half, rs_near, rs_two, agg, pbuf, mbuf, wbuf, obuf,
    load_sem, core_sem, y1s, y1r, y2s, y2r, y3s, y3r, rss, rsr, ms, mr, bs, br, group_sem,
):
    ny, nzl, nx, nc = dims
    nxc = nx * nc
    nq = nzl * nx
    rows = SLAB // (2 * ny)
    tokens = act_hbm.shape[0]
    piece = tokens // nx
    dp, tile = lax.axis_index("dp"), lax.axis_index("tile")
    zh, y = dp // ny, dp % ny
    zl, xc = tile // nxc, tile % nxc
    x, core = xc // nc, xc % nc
    q = zl * nx + x
    sent = []

    def at(zh_, y_, zl_, xc_):
        return (zh_ * ny + y_, zl_ * nxc + xc_)

    def xc_peer(k):
        return at(zh, y, zl, (xc + k) % nxc)

    def z_peer(k):
        return at(zh, y, (zl + k) % nzl, xc)

    def y_peer(k):
        return at(zh, (y + k + ny) % ny, zl, xc)

    def q_peer(a, k):
        far = (q + k) % nq
        return at((zh + a) % 2, y, far // nx, far % nx * nc + core)

    def remote(src, dst, send, recv, peer):
        copy = pltpu.make_async_remote_copy(
            src_ref=src, dst_ref=dst, send_sem=send, recv_sem=recv, device_id=peer, device_id_type=MESH
        )
        copy.start()
        return copy

    def kept(*args):
        sent.append(remote(*args))
        return sent[-1]

    load_bits = pltpu.make_async_copy(bits_hbm, bits_ref, load_sem.at[3])
    load_x = pltpu.make_async_copy(act_hbm, x_buf, load_sem.at[0])
    load_a = pltpu.make_async_copy(fac_hbm.at[:, pl.ds(0, SLAB)], fac_buf.at[:, pl.ds(0, SLAB)], load_sem.at[1])
    load_b = pltpu.make_async_copy(
        fac_hbm.at[:, pl.ds(SLAB, WIDTH - SLAB)], fac_buf.at[:, pl.ds(SLAB, WIDTH - SLAB)], load_sem.at[2]
    )
    load_bits.start()
    load_x.start()
    load_a.start()
    load_b.start()

    barrier = pltpu.get_barrier_semaphore()
    peers = [xc_peer(k) for k in range(1, nxc)] + [z_peer(k) for k in range(1, nzl)]
    peers += [y_peer(k) for k in (1, -1, 2, -2)]
    for peer in peers:
        pl.semaphore_signal(barrier, inc=1, device_id=peer, device_id_type=MESH)

    @pl.when(zl == 0)
    def _():
        pl.semaphore_signal(barrier, inc=1, device_id=at(1 - zh, y, nzl - 1, xc), device_id_type=MESH)

    col = lax.broadcasted_iota(jnp.int32, (1, WIDTH), 1)
    b_of = col - KF * ((col * 20165) >> 18)
    load_bits.wait()
    vee = jnp.zeros((1, WIDTH), F32)
    for b in range(KF):
        vee = jnp.where(b_of == b, (1 - 2 * bits_ref[b]).astype(F32), vee)
    flip = ((1 - 2 * sign_ref[...].reshape(1, WIDTH)).astype(F32) * vee).astype(BF)

    load_x.wait()
    x_buf[...] = x_buf[...] * flip
    load_a.wait()

    part = jnp.dot(x_buf[...], fac_buf[:, :SLAB], preferred_element_type=F32) * vee[:, :SLAB]
    inner[:, :SLAB] = part.astype(BF)
    for ix in range(nx):
        for ic in range(2):
            ysend[ix * 2 + ic] = part[ix * piece:(ix + 1) * piece, ic * LANES:(ic + 1) * LANES].astype(BF)
    pl.semaphore_wait(barrier, len(peers) + jnp.where(zl == nzl - 1, 1, 0))

    moves = [
        kept(ysend.at[(xc + k) % nxc], yrecv.at[k], y1s.at[k], y1r.at[k], xc_peer(k)) for k in range(1, nxc)
    ]
    load_b.wait()
    for c0 in range(SLAB, WIDTH, 256):
        c1 = min(c0 + 256, WIDTH)
        got = jnp.dot(x_buf[...], fac_buf[:, c0:c1], preferred_element_type=F32) * vee[:, c0:c1]
        inner[:, c0:c1] = got.astype(BF)
    core_move = kept(inner, other, core_sem.at[0], core_sem.at[1], at(zh, y, zl, x * nc + 1 - core))
    total = ysend[xc].astype(F32)
    for k in range(1, nxc):
        moves[k - 1].wait_recv()
        total = total + yrecv[k].astype(F32)
    ymid[...] = total.astype(BF)
    moves2 = [kept(ymid, yzrecv.at[k], y2s.at[k], y2r.at[k], z_peer(k)) for k in range(1, nzl)]
    total = ymid[...].astype(F32)
    for k in range(1, nzl):
        moves2[k - 1].wait_recv()
        total = total + yzrecv[k].astype(F32)
    yfull[xc] = total.astype(BF)
    moves3 = [
        kept(yfull.at[xc], yfull.at[xc], y3s.at[k], y3r.at[k], xc_peer(k)) for k in range(1, nxc)
    ]

    core_move.wait_recv()
    core_sign = (1 - 2 * core).astype(F32)
    other[...] = (other[...].astype(F32) + inner[...].astype(F32) * core_sign).astype(BF)
    for move in moves3:
        move.wait_recv()

    @pl.when(zl == nzl - 1)
    def _():
        pl.semaphore_signal(group_sem, inc=1, device_id=at(1 - zh, y, 0, xc), device_id_type=MESH)

    for half in range(2):
        left = jnp.concatenate([yfull[ix * 2 + half] for ix in range(nx)], axis=0)
        for c0 in range(0, WIDTH, 256):
            c1 = min(c0 + 256, WIDTH)
            got = lax.dot_general(
                left, other[:, c0:c1], (((0,), (0,)), ((), ())), preferred_element_type=F32
            ).astype(BF)
            for iy in range(ny):
                for j in range((c1 - c0) // LANES):
                    gp[iy, c0 // LANES + j, half] = got[iy * rows:(iy + 1) * rows, j * LANES:(j + 1) * LANES]

    chunks = [(NT * m // CHUNKS, NT * (m + 1) // CHUNKS) for m in range(CHUNKS)]
    ways = (1, -1)
    aggs, halves, nears, twos = {}, {}, {}, {}

    def index(kind, way, m):
        return (kind * 2 + (way + 1) // 2) * CHUNKS + m

    def block(to, m):
        lo, hi = chunks[m]
        return gp.at[(y + to + ny) % ny, pl.ds(lo, hi - lo)]

    def slot(ref, way, m):
        lo, hi = chunks[m]
        return ref.at[(way + 1) // 2, pl.ds(lo, hi - lo)]

    def y_send(kind, src, ref, way, m, to):
        n = index(kind, way, m)
        return kept(src, slot(ref, way, m), rss.at[n], rsr.at[n], y_peer(to))

    for m in range(CHUNKS):
        lo, hi = chunks[m]
        for way in ways:
            n = index(1, way, m)
            side = (way + 1) // 2
            halves[way, m] = kept(
                gp.at[(y + ny // 2) % ny, pl.ds(lo, hi - lo), side], slot(rs_half, way, m),
                rss.at[n], rsr.at[n], y_peer(2 * way),
            )
        for way in ways:
            aggs[way, m] = y_send(0, block(3 * way, m), rs_agg, way, m, way)
    for m in range(CHUNKS):
        for way in ways:
            nears[way, m] = y_send(2, block(way, m), rs_near, way, m, way)
    for m in range(CHUNKS):
        lo, hi = chunks[m]
        for way in ways:
            side = (way + 1) // 2
            aggs[way, m].wait_recv()
            halves[way, m].wait_recv()
            for h in range(2):
                total = block(2 * way, m)[:, h].astype(F32) + rs_agg[side, lo:hi, h].astype(F32)
                if h == side:
                    total = total + rs_half[side, lo:hi].astype(F32)
                agg[side, lo:hi, h] = total.astype(BF)
            twos[way, m] = y_send(3, slot(agg, way, m), rs_two, way, m, 2 * way)

    @pl.when(zl == 0)
    def _():
        pl.semaphore_wait(group_sem, 1)
        for k in range(1, nzl):
            pl.semaphore_signal(group_sem, inc=1, device_id=z_peer(k), device_id_type=MESH)

    @pl.when(zl != 0)
    def _():
        pl.semaphore_wait(group_sem, 1)

    for m in range(CHUNKS):
        lo, hi = chunks[m]
        for way in ways:
            nears[way, m].wait_recv()
            twos[way, m].wait_recv()
        for h in range(2):
            total = block(0, m)[:, h].astype(F32)
            for side in range(2):
                total = total + rs_near[side, lo:hi, h].astype(F32) + rs_two[side, lo:hi, h].astype(F32)
            pbuf[h, lo:hi] = total.astype(BF)

    hops = [(a, k) for a in range(2) for k in range(nq) if (a, k) != (0, 0)]

    def mix_move(a, k):
        far = (q + k) % nq
        return pltpu.make_async_remote_copy(
            src_ref=pbuf.at[(zh + a) % 2, far], dst_ref=mbuf.at[zh * nq + q],
            send_sem=ms, recv_sem=mr, device_id=q_peer(a, k), device_id_type=MESH,
        )

    for a, k in hops:
        @pl.when((q + k) % nq < NT)
        def _():
            mix_move(a, k).start()

    def back_move(k):
        return pltpu.make_async_remote_copy(
            src_ref=wbuf.at[(q + k) % nq], dst_ref=obuf.at[q],
            send_sem=bs, recv_sem=br, device_id=q_peer(0, k), device_id_type=MESH,
        )

    def drain(ref, count, sem):
        part = ref.at[pl.ds(0, count)]
        pltpu.make_async_copy(part, part, sem).wait()

    @pl.when(q < NT)
    def _():
        mbuf[zh * nq + q] = pbuf[zh, q]
        drain(mbuf, 2 * nq - 1, mr)
        mixed = butterfly([mbuf[l].astype(F32) + mbuf[nq + l].astype(F32) for l in range(nq)])
        for l in range(nq):
            wbuf[l] = mixed[l].astype(BF)
        for k in range(1, nq):
            back_move(k).start()
        obuf[q] = wbuf[q]
        drain(obuf, NT - 1, br)
        drain(wbuf, nq - 1, bs)
        drain(mbuf, 2 * NT - 1, ms)

    @pl.when(q >= NT)
    def _():
        drain(obuf, NT, br)
        drain(mbuf, 2 * NT, ms)

    for j in range(NT):
        out_ref[:, j * LANES:(j + 1) * LANES] = obuf[j].astype(F32)
    for move in sent:
        move.wait_send()


def shards(dims, activations, sign_bits, factor_bits):
    ny, nzl, nx, nc = dims
    nxc = nx * nc
    nq = nzl * nx
    rows = SLAB // (2 * ny)
    tokens = activations.shape[0]
    piece = tokens // nx
    dma = pltpu.SemaphoreType.DMA
    vm = pltpu.VMEM
    gram = pl.pallas_call(
        functools.partial(kernel, dims),
        out_shape=jax.ShapeDtypeStruct((rows, WIDTH), F32),
        in_specs=[
            pl.BlockSpec(memory_space=pl.ANY),
            pl.BlockSpec(memory_space=pltpu.VMEM),
            pl.BlockSpec(memory_space=pl.ANY),
            pl.BlockSpec(memory_space=pl.ANY),
        ],
        out_specs=pl.BlockSpec(memory_space=pltpu.VMEM),
        scratch_shapes=[
            vm((tokens, WIDTH), BF),
            vm((WIDTH, WIDTH), BF),
            vm((tokens, WIDTH), BF),
            vm((tokens, WIDTH), BF),
            pltpu.SMEM((KF,), jnp.int32),
            vm((nxc, piece, LANES), BF),
            vm((nxc, piece, LANES), BF),
            vm((piece, LANES), BF),
            vm((nzl, piece, LANES), BF),
            vm((nxc, piece, LANES), BF),
            vm((ny, NT, 2, rows, LANES), BF),
            vm((2, NT, 2, rows, LANES), BF),
            vm((2, NT, rows, LANES), BF),
            vm((2, NT, 2, rows, LANES), BF),
            vm((2, NT, 2, rows, LANES), BF),
            vm((2, NT, 2, rows, LANES), BF),
            vm((2, NT, rows, LANES), BF),
            vm((2 * nq, rows, LANES), BF),
            vm((nq, rows, LANES), BF),
            vm((NT, rows, LANES), BF),
            dma((4,)),
            dma((2,)),
            dma((nxc,)), dma((nxc,)),
            dma((nzl,)), dma((nzl,)),
            dma((nxc,)), dma((nxc,)),
            dma((8 * CHUNKS,)), dma((8 * CHUNKS,)),
            dma, dma,
            dma, dma,
            pltpu.SemaphoreType.REGULAR,
        ],
        compiler_params=pltpu.CompilerParams(
            collective_id=0, has_side_effects=True, vmem_limit_bytes=VMEM_LIMIT
        ),
    )(activations, sign_bits, factor_bits, jnp.asarray(small_factor()))
    row = lax.axis_index("dp") * rows + lax.broadcasted_iota(jnp.int32, gram.shape, 0)
    col = lax.axis_index("tile") * WIDTH + lax.broadcasted_iota(jnp.int32, gram.shape, 1)
    keep = col // LANES >= row // LANES
    all_tokens = tokens * 2 * ny
    return jnp.where(keep, gram * (2.0 / all_tokens / HAD), 0.0)


def solution(mesh, dims=(8, 4, 4, 2)):
    return jax.shard_map(
        functools.partial(shards, dims),
        mesh=mesh,
        in_specs=(P("dp", "tile"), P("tile"), P()),
        out_specs=P("dp", "tile"),
        check_vma=False,
    )
```

```python
import functools

import jax
import jax.numpy as jnp
import ml_dtypes
import numpy as np
from jax import lax
from jax.experimental import pallas as pl
from jax.experimental.pallas import tpu as pltpu
from jax.sharding import PartitionSpec as P

KF = 13
HB = 128
WIDTH = KF * HB
SLAB = 256
HAD = 4096
LANES = 128
NT = WIDTH // LANES
ORDER = (10, 6, 14, 9, 11, 5, 7, 13, 15, 2, 8, 1, 3, 4, 12)
CUTS = (0, 4, 8, 13)
CHUNKS = len(CUTS) - 1
THREE = (True, True, False)
SPLIT = 1280
VMEM_LIMIT = 60 * 1024 * 1024
MESH = pl.DeviceIdType.MESH
BF = jnp.bfloat16
F32 = jnp.float32


def small_factor():
    index = np.arange(HB)
    both = index[:, None] & index[None, :]
    parity = np.zeros_like(both)
    for shift in range(7):
        parity ^= (both >> shift) & 1
    hblock = (1 - 2 * parity).astype(np.float32)
    refl = np.eye(KF, dtype=np.float32) - np.float32(2.0 / KF)
    return np.kron(hblock, refl).astype(ml_dtypes.bfloat16)


def butterfly(parts):
    step = 1
    parts = list(parts)
    while step < len(parts):
        for low in range(len(parts)):
            if not low & step:
                a, b = parts[low], parts[low | step]
                parts[low], parts[low | step] = a + b, a - b
        step *= 2
    return parts


def kernel(
    dims,
    act_hbm, sign_hbm, bits_hbm, fac_hbm,
    out_ref,
    x_buf, fac_buf, inner, other, sign_ref, bits_ref, ysend, yrecv, ymid, yzrecv, yfull,
    gp, rs_agg, rs_half, rs_near, rs_two, agg, pbuf, mbuf, wbuf,
    load_sem, core_sem, y1s, y1r, y2s, y2r, y3s, y3r, rss, rsr, ms, mr, bs, br, group_sem,
):
    ny, nzl, nx, nc = dims
    nxc = nx * nc
    nq = nzl * nx
    rows = SLAB // (2 * ny)
    tokens = act_hbm.shape[0]
    piece = tokens // nx
    dp, tile = lax.axis_index("dp"), lax.axis_index("tile")
    zh, y = dp // ny, dp % ny
    zl, xc = tile // nxc, tile % nxc
    x, core = xc // nc, xc % nc
    q = zl * nx + x
    mine = (q + nq // 2 * core) % nq
    sent = []

    def at(zh_, y_, zl_, xc_):
        return (zh_ * ny + y_, zl_ * nxc + xc_)

    def xc_peer(k):
        return at(zh, y, zl, (xc + k) % nxc)

    def z_peer(k):
        return at(zh, y, (zl + k) % nzl, xc)

    def y_peer(k):
        return at(zh, (y + k + ny) % ny, zl, xc)

    def q_peer(k):
        far = (q + k) % nq
        return at(zh, y, far // nx, far % nx * nc + core)

    def remote(src, dst, send, recv, peer):
        copy = pltpu.make_async_remote_copy(
            src_ref=src, dst_ref=dst, send_sem=send, recv_sem=recv, device_id=peer, device_id_type=MESH
        )
        copy.start()
        return copy

    def kept(*args):
        sent.append(remote(*args))
        return sent[-1]

    def settle():
        for copy in sent:
            copy.wait_send()
        sent.clear()

    load_bits = pltpu.make_async_copy(bits_hbm, bits_ref, load_sem.at[3])
    load_x = pltpu.make_async_copy(act_hbm, x_buf, load_sem.at[0])
    load_a = pltpu.make_async_copy(fac_hbm.at[:, pl.ds(0, SLAB)], fac_buf.at[:, pl.ds(0, SLAB)], load_sem.at[1])
    load_b = pltpu.make_async_copy(
        fac_hbm.at[:, pl.ds(SLAB, WIDTH - SLAB)], fac_buf.at[:, pl.ds(SLAB, WIDTH - SLAB)], load_sem.at[2]
    )
    load_sign = pltpu.make_async_copy(sign_hbm, sign_ref, load_sem.at[4])
    load_x.start()
    load_a.start()
    load_sign.start()
    load_bits.start()
    load_b.start()

    barrier = pltpu.get_barrier_semaphore()
    peers = [xc_peer(k) for k in range(1, nxc)] + [z_peer(k) for k in range(1, nzl)]
    peers += [y_peer(k) for k in (1, -1, 2, -2)]
    for peer in peers:
        pl.semaphore_signal(barrier, inc=1, device_id=peer, device_id_type=MESH)

    @pl.when(zl == 0)
    def _():
        pl.semaphore_signal(barrier, inc=1, device_id=at(1 - zh, y, nzl - 1, xc), device_id_type=MESH)

    col = lax.broadcasted_iota(jnp.int32, (1, WIDTH), 1)
    b_of = col - KF * ((col * 20165) >> 18)
    load_sign.wait()
    load_bits.wait()
    vee = jnp.zeros((1, WIDTH), F32)
    for b in range(KF):
        vee = jnp.where(b_of == b, (1 - 2 * bits_ref[b]).astype(F32), vee)
    flip = ((1 - 2 * sign_ref[...].reshape(1, WIDTH)).astype(F32) * vee).astype(BF)

    load_x.wait()
    x_buf[...] = x_buf[...] * flip
    load_a.wait()

    part = jnp.dot(x_buf[...], fac_buf[:, :SLAB], preferred_element_type=F32) * vee[:, :SLAB]
    inner[:, :SLAB] = part.astype(BF)
    for ix in range(nx):
        for ic in range(2):
            ysend[ix * 2 + ic] = part[ix * piece:(ix + 1) * piece, ic * LANES:(ic + 1) * LANES].astype(BF)
    pl.semaphore_wait(barrier, len(peers) + jnp.where(zl == nzl - 1, 1, 0))

    def more_inner(first, last):
        for c0 in range(first, last, 256):
            c1 = min(c0 + 256, last)
            got = jnp.dot(x_buf[...], fac_buf[:, c0:c1], preferred_element_type=F32) * vee[:, c0:c1]
            inner[:, c0:c1] = got.astype(BF)

    def swap_cores(n, first, last):
        part = pl.ds(first, last - first)
        return kept(
            inner.at[:, part], other.at[:, part], core_sem.at[n], core_sem.at[2 + n], at(zh, y, zl, x * nc + 1 - core)
        )

    def mix_cores(n, first, last):
        core_moves[n].wait_recv()
        sign = (1 - 2 * core).astype(F32)
        other[:, first:last] = (
            other[:, first:last].astype(F32) + inner[:, first:last].astype(F32) * sign
        ).astype(BF)

    moves = [
        kept(ysend.at[(xc + k) % nxc], yrecv.at[k], y1s.at[k], y1r.at[k], xc_peer(k)) for k in range(1, nxc)
    ]
    load_b.wait()
    more_inner(SLAB, SPLIT)
    core_moves = [swap_cores(0, 0, SPLIT)]
    total = ysend[xc].astype(F32)
    for k in range(1, nxc):
        moves[k - 1].wait_recv()
        total = total + yrecv[k].astype(F32)
    ymid[...] = total.astype(BF)
    moves2 = [kept(ymid, yzrecv.at[k], y2s.at[k], y2r.at[k], z_peer(k)) for k in range(1, nzl)]
    more_inner(SPLIT, WIDTH)
    core_moves.append(swap_cores(1, SPLIT, WIDTH))
    mix_cores(0, 0, SPLIT)
    total = ymid[...].astype(F32)
    for k in range(1, nzl):
        moves2[k - 1].wait_recv()
        total = total + yzrecv[k].astype(F32)
    yfull[xc] = total.astype(BF)
    moves3 = [
        kept(yfull.at[xc], yfull.at[xc], y3s.at[k], y3r.at[k], xc_peer(k)) for k in range(1, nxc)
    ]

    mix_cores(1, SPLIT, WIDTH)
    for move in moves3:
        move.wait_recv()

    @pl.when(zl == nzl - 1)
    def _():
        pl.semaphore_signal(group_sem, inc=1, device_id=at(1 - zh, y, 0, xc), device_id_type=MESH)

    lefts = [jnp.concatenate([yfull[ix * 2 + half] for ix in range(nx)], axis=0).T for half in range(2)]

    def gram_terms(first, last):
        for c0 in range(first * LANES, last * LANES, 256):
            c1 = min(c0 + 256, last * LANES)
            for half in range(2):
                got = jnp.dot(lefts[half], other[:, c0:c1], preferred_element_type=F32).astype(BF)
                for iy in range(ny):
                    for j in range((c1 - c0) // LANES):
                        gp[iy, c0 // LANES + j, half] = got[iy * rows:(iy + 1) * rows, j * LANES:(j + 1) * LANES]

    chunks = list(zip(CUTS[:-1], CUTS[1:]))
    ways = (1, -1)
    aggs, halves, nears, twos = {}, {}, {}, {}

    def index(kind, way, m):
        return (kind * 2 + (way + 1) // 2) * CHUNKS + m

    def block(to, m):
        lo, hi = chunks[m]
        return gp.at[(y + to + ny) % ny, pl.ds(lo, hi - lo)]

    def slot(ref, way, m):
        lo, hi = chunks[m]
        return ref.at[(way + 1) // 2, pl.ds(lo, hi - lo)]

    def y_send(kind, src, ref, way, m, to):
        n = index(kind, way, m)
        return kept(src, slot(ref, way, m), rss.at[n], rsr.at[n], y_peer(to))

    for m in range(CHUNKS):
        lo, hi = chunks[m]
        gram_terms(lo, hi)
        for way in ways:
            n = index(1, way, m)
            side = (way + 1) // 2
            halves[way, m] = kept(
                gp.at[(y + ny // 2) % ny, pl.ds(lo, hi - lo), side], slot(rs_half, way, m),
                rss.at[n], rsr.at[n], y_peer(2 * way),
            )
        for way in ways:
            aggs[way, m] = y_send(0, block(3 * way, m), rs_agg, way, m, way)
    for m in range(CHUNKS):
        if not THREE[m]:
            for way in ways:
                nears[way, m] = y_send(2, block(way, m), rs_near, way, m, way)
    for m in range(CHUNKS):
        lo, hi = chunks[m]
        for way in ways:
            side = (way + 1) // 2
            aggs[way, m].wait_recv()
            halves[way, m].wait_recv()
            for h in range(2):
                total = block(2 * way, m)[:, h].astype(F32) + rs_agg[side, lo:hi, h].astype(F32)
                if h == side:
                    total = total + rs_half[side, lo:hi].astype(F32)
                agg[side, lo:hi, h] = total.astype(BF)
            twos[way, m] = y_send(3, slot(agg, way, m), rs_two, way, m, way if THREE[m] else 2 * way)
    for m in range(CHUNKS):
        if THREE[m]:
            lo, hi = chunks[m]
            for way in ways:
                side = (way + 1) // 2
                twos[way, m].wait_recv()
                rs_two[side, lo:hi] = (rs_two[side, lo:hi].astype(F32) + block(way, m)[...].astype(F32)).astype(BF)
                nears[way, m] = y_send(2, slot(rs_two, way, m), rs_near, way, m, way)

    @pl.when(zl == 0)
    def _():
        pl.semaphore_wait(group_sem, 1)
        for k in range(1, nzl):
            pl.semaphore_signal(group_sem, inc=1, device_id=z_peer(k), device_id_type=MESH)

    @pl.when(zl != 0)
    def _():
        pl.semaphore_wait(group_sem, 1)

    def mix_move(a, p):
        return pltpu.make_async_remote_copy(
            src_ref=pbuf.at[(zh + a) % 2, p], dst_ref=mbuf.at[zh * nq + q], send_sem=ms, recv_sem=mr,
            device_id=at((zh + a) % 2, y, (p // nx + nzl // 2 * core) % nzl, p % nx * nc + core),
            device_id_type=MESH,
        )

    for m in range(CHUNKS):
        lo, hi = chunks[m]
        for way in ways:
            nears[way, m].wait_recv()
            if not THREE[m]:
                twos[way, m].wait_recv()
        for h in range(2):
            total = block(0, m)[:, h].astype(F32)
            for side in range(2):
                total = total + rs_near[side, lo:hi, h].astype(F32)
                if not THREE[m]:
                    total = total + rs_two[side, lo:hi, h].astype(F32)
            pbuf[h, lo:hi] = total.astype(BF)
        for p in range(lo, hi):
            mix_move(1, p).start()
        for p in range(lo, hi):
            @pl.when(mine != p)
            def _():
                mix_move(0, p).start()

    settle()

    def back_move(k):
        return pltpu.make_async_remote_copy(
            src_ref=wbuf.at[(q + k) % nq], dst_ref=out_ref.at[:, pl.ds(pl.multiple_of(mine * LANES, LANES), LANES)],
            send_sem=bs, recv_sem=br, device_id=q_peer(k), device_id_type=MESH,
        )

    def drain(ref, count, sem):
        part = ref.at[pl.ds(0, count)]
        pltpu.make_async_copy(part, part, sem).wait()

    @pl.when(mine < NT)
    def _():
        mbuf[zh * nq + q] = pbuf[zh, mine]
        drain(mbuf, 2 * nq - 1, mr)
        mixed = butterfly([mbuf[l].astype(F32) + mbuf[nq + l].astype(F32) for l in range(nq)])
        for l in range(nq):
            wbuf[l] = mixed[l].astype(BF)
        for k in ORDER:
            back_move(k).start()
        own = pltpu.make_async_copy(
            wbuf.at[q], out_ref.at[:, pl.ds(pl.multiple_of(mine * LANES, LANES), LANES)], load_sem.at[5]
        )
        own.start()
        drain(mbuf, 2 * NT - 1, ms)
        own.wait()
        drain(mbuf, NT - 1, br)
        drain(wbuf, nq - 1, bs)

    @pl.when(mine >= NT)
    def _():
        drain(mbuf, 2 * NT, ms)
        drain(mbuf, NT, br)


def shards(dims, activations, sign_bits, factor_bits):
    ny, nzl, nx, nc = dims
    nxc = nx * nc
    nq = nzl * nx
    rows = SLAB // (2 * ny)
    tokens = activations.shape[0]
    piece = tokens // nx
    dma = pltpu.SemaphoreType.DMA
    vm = pltpu.VMEM
    gram = pl.pallas_call(
        functools.partial(kernel, dims),
        out_shape=jax.ShapeDtypeStruct((rows, WIDTH), BF),
        in_specs=[
            pl.BlockSpec(memory_space=pl.ANY),
            pl.BlockSpec(memory_space=pl.ANY),
            pl.BlockSpec(memory_space=pl.ANY),
            pl.BlockSpec(memory_space=pl.ANY),
        ],
        out_specs=pl.BlockSpec(memory_space=pl.ANY),
        scratch_shapes=[
            vm((tokens, WIDTH), BF),
            vm((WIDTH, WIDTH), BF),
            vm((tokens, WIDTH), BF),
            vm((tokens, WIDTH), BF),
            vm((WIDTH,), jnp.int32),
            pltpu.SMEM((KF,), jnp.int32),
            vm((nxc, piece, LANES), BF),
            vm((nxc, piece, LANES), BF),
            vm((piece, LANES), BF),
            vm((nzl, piece, LANES), BF),
            vm((nxc, piece, LANES), BF),
            vm((ny, NT, 2, rows, LANES), BF),
            vm((2, NT, 2, rows, LANES), BF),
            vm((2, NT, rows, LANES), BF),
            vm((2, NT, 2, rows, LANES), BF),
            vm((2, NT, 2, rows, LANES), BF),
            vm((2, NT, 2, rows, LANES), BF),
            vm((2, NT, rows, LANES), BF),
            vm((2 * nq, rows, LANES), BF),
            vm((nq, rows, LANES), BF),
            dma((6,)),
            dma((4,)),
            dma((nxc,)), dma((nxc,)),
            dma((nzl,)), dma((nzl,)),
            dma((nxc,)), dma((nxc,)),
            dma((8 * CHUNKS,)), dma((8 * CHUNKS,)),
            dma, dma,
            dma, dma,
            pltpu.SemaphoreType.REGULAR,
        ],
        compiler_params=pltpu.CompilerParams(
            collective_id=0, has_side_effects=True, vmem_limit_bytes=VMEM_LIMIT
        ),
    )(activations, sign_bits, factor_bits, jnp.asarray(small_factor()))
    row = lax.axis_index("dp") * rows + lax.broadcasted_iota(jnp.int32, gram.shape, 0)
    col = lax.axis_index("tile") * WIDTH + lax.broadcasted_iota(jnp.int32, gram.shape, 1)
    keep = col // LANES >= row // LANES
    all_tokens = tokens * 2 * ny
    return jnp.where(keep, gram.astype(F32) * (2.0 / all_tokens / HAD), 0.0)


def solution(mesh, dims=(8, 4, 4, 2)):
    return jax.shard_map(
        functools.partial(shards, dims),
        mesh=mesh,
        in_specs=(P("dp", "tile"), P("tile"), P()),
        out_specs=P("dp", "tile"),
        check_vma=False,
    )
```

```python
import functools

import jax
import jax.numpy as jnp
import ml_dtypes
import numpy as np
from jax import lax
from jax.experimental import pallas as pl
from jax.experimental.pallas import tpu as pltpu
from jax.sharding import PartitionSpec as P

KF = 13
HB = 128
WIDTH = KF * HB
SLAB = 256
HAD = 4096
LANES = 128
NT = WIDTH // LANES
NU = (NT + 1) // 2
BACK = ((2, 2), (1, 2), (3, 2), (2, 1), (2, 3), (1, 1), (1, 3), (3, 1), (3, 3), (2, 0), (0, 2), (1, 0), (3, 0), (0, 1), (0, 3))
CUTS = (0, 4, 8, 13)
CHUNKS = len(CUTS) - 1
THREE = (True, True, False)
SPLIT = 1280
VMEM_LIMIT = 60 * 1024 * 1024
MESH = pl.DeviceIdType.MESH
BF = jnp.bfloat16
F32 = jnp.float32


def small_factor():
    index = np.arange(HB)
    both = index[:, None] & index[None, :]
    parity = np.zeros_like(both)
    for shift in range(7):
        parity ^= (both >> shift) & 1
    hblock = (1 - 2 * parity).astype(np.float32)
    refl = np.eye(KF, dtype=np.float32) - np.float32(2.0 / KF)
    return np.kron(hblock, refl).astype(ml_dtypes.bfloat16)


def butterfly(parts):
    step = 1
    parts = list(parts)
    while step < len(parts):
        for low in range(len(parts)):
            if not low & step:
                a, b = parts[low], parts[low | step]
                parts[low], parts[low | step] = a + b, a - b
        step *= 2
    return parts


def kernel(
    dims,
    act_hbm, sign_hbm, bits_hbm, fac_hbm,
    out_ref,
    x_buf, fac_buf, inner, other, sign_ref, bits_ref, ysend, yrecv, ymid, yzrecv, yfull,
    gp, rs_agg, rs_half, rs_near, rs_two, agg, pbuf, mbuf, wbuf,
    load_sem, core_sem, y1s, y1r, y2s, y2r, y3s, y3r, rss, rsr, ms, mr, bs, br, group_sem,
):
    ny, nzl, nx, nc = dims
    nxc = nx * nc
    nq = nzl * nx
    rows = SLAB // (2 * ny)
    tokens = act_hbm.shape[0]
    piece = tokens // nx
    dp, tile = lax.axis_index("dp"), lax.axis_index("tile")
    zh, y = dp // ny, dp % ny
    zl, xc = tile // nxc, tile % nxc
    x, core = xc // nc, xc % nc
    q = zl * nx + x
    middle = (zl + 1) // 2 % 2
    mine = ((zl - 1) * nx + x + nx * core + 2 * nx) % (2 * nx)
    owner_here = middle * jnp.where(mine < NU, 1, 0) == 1
    sent = []

    def at(zh_, y_, zl_, xc_):
        return (zh_ * ny + y_, zl_ * nxc + xc_)

    def xc_peer(k):
        return at(zh, y, zl, (xc + k) % nxc)

    def z_peer(k):
        return at(zh, y, (zl + k) % nzl, xc)

    def y_peer(k):
        return at(zh, (y + k + ny) % ny, zl, xc)

    def q_peer(k):
        far = (q + k) % nq
        return at(zh, y, far // nx, far % nx * nc + core)

    def remote(src, dst, send, recv, peer):
        copy = pltpu.make_async_remote_copy(
            src_ref=src, dst_ref=dst, send_sem=send, recv_sem=recv, device_id=peer, device_id_type=MESH
        )
        copy.start()
        return copy

    def kept(*args):
        sent.append(remote(*args))
        return sent[-1]

    def settle():
        for copy in sent:
            copy.wait_send()
        sent.clear()

    load_bits = pltpu.make_async_copy(bits_hbm, bits_ref, load_sem.at[3])
    load_x = pltpu.make_async_copy(act_hbm, x_buf, load_sem.at[0])
    load_a = pltpu.make_async_copy(fac_hbm.at[:, pl.ds(0, SLAB)], fac_buf.at[:, pl.ds(0, SLAB)], load_sem.at[1])
    load_b = pltpu.make_async_copy(
        fac_hbm.at[:, pl.ds(SLAB, WIDTH - SLAB)], fac_buf.at[:, pl.ds(SLAB, WIDTH - SLAB)], load_sem.at[2]
    )
    load_sign = pltpu.make_async_copy(sign_hbm, sign_ref, load_sem.at[4])
    load_x.start()
    load_a.start()
    load_sign.start()
    load_bits.start()
    load_b.start()

    barrier = pltpu.get_barrier_semaphore()
    peers = [xc_peer(k) for k in range(1, nxc)] + [z_peer(k) for k in range(1, nzl)]
    peers += [y_peer(k) for k in (1, -1, 2, -2)]
    for peer in peers:
        pl.semaphore_signal(barrier, inc=1, device_id=peer, device_id_type=MESH)

    @pl.when(zl == 0)
    def _():
        pl.semaphore_signal(barrier, inc=1, device_id=at(1 - zh, y, nzl - 1, xc), device_id_type=MESH)

    col = lax.broadcasted_iota(jnp.int32, (1, WIDTH), 1)
    b_of = col - KF * ((col * 20165) >> 18)
    load_sign.wait()
    load_bits.wait()
    vee = jnp.zeros((1, WIDTH), F32)
    for b in range(KF):
        vee = jnp.where(b_of == b, (1 - 2 * bits_ref[b]).astype(F32), vee)
    flip = ((1 - 2 * sign_ref[...].reshape(1, WIDTH)).astype(F32) * vee).astype(BF)

    load_x.wait()
    x_buf[...] = x_buf[...] * flip
    load_a.wait()

    part = jnp.dot(x_buf[...], fac_buf[:, :SLAB], preferred_element_type=F32) * vee[:, :SLAB]
    inner[:, :SLAB] = part.astype(BF)
    for ix in range(nx):
        for ic in range(2):
            ysend[ix * 2 + ic] = part[ix * piece:(ix + 1) * piece, ic * LANES:(ic + 1) * LANES].astype(BF)
    pl.semaphore_wait(barrier, len(peers) + jnp.where(zl == nzl - 1, 1, 0))

    def more_inner(first, last):
        for c0 in range(first, last, 256):
            c1 = min(c0 + 256, last)
            got = jnp.dot(x_buf[...], fac_buf[:, c0:c1], preferred_element_type=F32) * vee[:, c0:c1]
            inner[:, c0:c1] = got.astype(BF)

    def swap_cores(n, first, last):
        part = pl.ds(first, last - first)
        return kept(
            inner.at[:, part], other.at[:, part], core_sem.at[n], core_sem.at[2 + n], at(zh, y, zl, x * nc + 1 - core)
        )

    def mix_cores(n, first, last):
        core_moves[n].wait_recv()
        sign = (1 - 2 * core).astype(F32)
        other[:, first:last] = (
            other[:, first:last].astype(F32) + inner[:, first:last].astype(F32) * sign
        ).astype(BF)

    moves = [
        kept(ysend.at[(xc + k) % nxc], yrecv.at[k], y1s.at[k], y1r.at[k], xc_peer(k)) for k in range(1, nxc)
    ]
    load_b.wait()
    more_inner(SLAB, SPLIT)
    core_moves = [swap_cores(0, 0, SPLIT)]
    total = ysend[xc].astype(F32)
    for k in range(1, nxc):
        moves[k - 1].wait_recv()
        total = total + yrecv[k].astype(F32)
    ymid[...] = total.astype(BF)
    moves2 = [kept(ymid, yzrecv.at[k], y2s.at[k], y2r.at[k], z_peer(k)) for k in range(1, nzl)]
    more_inner(SPLIT, WIDTH)
    core_moves.append(swap_cores(1, SPLIT, WIDTH))
    mix_cores(0, 0, SPLIT)
    total = ymid[...].astype(F32)
    for k in range(1, nzl):
        moves2[k - 1].wait_recv()
        total = total + yzrecv[k].astype(F32)
    yfull[xc] = total.astype(BF)
    moves3 = [
        kept(yfull.at[xc], yfull.at[xc], y3s.at[k], y3r.at[k], xc_peer(k)) for k in range(1, nxc)
    ]

    mix_cores(1, SPLIT, WIDTH)
    for move in moves3:
        move.wait_recv()

    @pl.when(zl == nzl - 1)
    def _():
        pl.semaphore_signal(group_sem, inc=1, device_id=at(1 - zh, y, 0, xc), device_id_type=MESH)

    lefts = [jnp.concatenate([yfull[ix * 2 + half] for ix in range(nx)], axis=0).T for half in range(2)]

    def gram_terms(first, last):
        for c0 in range(first * LANES, last * LANES, 256):
            c1 = min(c0 + 256, last * LANES)
            for half in range(2):
                got = jnp.dot(lefts[half], other[:, c0:c1], preferred_element_type=F32).astype(BF)
                for iy in range(ny):
                    for j in range((c1 - c0) // LANES):
                        gp[iy, c0 // LANES + j, half] = got[iy * rows:(iy + 1) * rows, j * LANES:(j + 1) * LANES]

    chunks = list(zip(CUTS[:-1], CUTS[1:]))
    ways = (1, -1)
    aggs, halves, nears, twos = {}, {}, {}, {}

    def index(kind, way, m):
        return (kind * 2 + (way + 1) // 2) * CHUNKS + m

    def block(to, m):
        lo, hi = chunks[m]
        return gp.at[(y + to + ny) % ny, pl.ds(lo, hi - lo)]

    def slot(ref, way, m):
        lo, hi = chunks[m]
        return ref.at[(way + 1) // 2, pl.ds(lo, hi - lo)]

    def y_send(kind, src, ref, way, m, to):
        n = index(kind, way, m)
        return kept(src, slot(ref, way, m), rss.at[n], rsr.at[n], y_peer(to))

    for m in range(CHUNKS):
        lo, hi = chunks[m]
        gram_terms(lo, hi)
        for way in ways:
            n = index(1, way, m)
            side = (way + 1) // 2
            halves[way, m] = kept(
                gp.at[(y + ny // 2) % ny, pl.ds(lo, hi - lo), side], slot(rs_half, way, m),
                rss.at[n], rsr.at[n], y_peer(2 * way),
            )
        for way in ways:
            aggs[way, m] = y_send(0, block(3 * way, m), rs_agg, way, m, way)
    for m in range(CHUNKS):
        if not THREE[m]:
            for way in ways:
                nears[way, m] = y_send(2, block(way, m), rs_near, way, m, way)
    for m in range(CHUNKS):
        lo, hi = chunks[m]
        for way in ways:
            side = (way + 1) // 2
            aggs[way, m].wait_recv()
            halves[way, m].wait_recv()
            for h in range(2):
                total = block(2 * way, m)[:, h].astype(F32) + rs_agg[side, lo:hi, h].astype(F32)
                if h == side:
                    total = total + rs_half[side, lo:hi].astype(F32)
                agg[side, lo:hi, h] = total.astype(BF)
            twos[way, m] = y_send(3, slot(agg, way, m), rs_two, way, m, way if THREE[m] else 2 * way)
    for m in range(CHUNKS):
        if THREE[m]:
            lo, hi = chunks[m]
            for way in ways:
                side = (way + 1) // 2
                twos[way, m].wait_recv()
                rs_two[side, lo:hi] = (rs_two[side, lo:hi].astype(F32) + block(way, m)[...].astype(F32)).astype(BF)
                nears[way, m] = y_send(2, slot(rs_two, way, m), rs_near, way, m, way)

    @pl.when(zl == 0)
    def _():
        pl.semaphore_wait(group_sem, 1)
        for k in range(1, nzl):
            pl.semaphore_signal(group_sem, inc=1, device_id=z_peer(k), device_id_type=MESH)

    @pl.when(zl != 0)
    def _():
        pl.semaphore_wait(group_sem, 1)

    def mix_move(a, u):
        spot = u + nx * core
        return pltpu.make_async_remote_copy(
            src_ref=pbuf.at[(zh + a) % 2, pl.ds(2 * u, 2)], dst_ref=mbuf.at[zh * nq + q], send_sem=ms, recv_sem=mr,
            device_id=at((zh + a) % 2, y, 1 + spot // nx % 2, spot % nx * nc + core),
            device_id_type=MESH,
        )

    for m in range(CHUNKS):
        lo, hi = chunks[m]
        for way in ways:
            nears[way, m].wait_recv()
            if not THREE[m]:
                twos[way, m].wait_recv()
        for h in range(2):
            total = block(0, m)[:, h].astype(F32)
            for side in range(2):
                total = total + rs_near[side, lo:hi, h].astype(F32)
                if not THREE[m]:
                    total = total + rs_two[side, lo:hi, h].astype(F32)
            pbuf[h, lo:hi] = total.astype(BF)
            if hi == NT:
                for j in range(NT, 2 * NU):
                    pbuf[h, j] = jnp.zeros((rows, LANES), BF)
        for u in range(lo // 2, (hi + 1) // 2):
            mix_move(1, u).start()
        for u in range(lo // 2, (hi + 1) // 2):
            @pl.when(jnp.logical_not(jnp.logical_and(owner_here, mine == u)))
            def _():
                mix_move(0, u).start()

    settle()

    def columns(u):
        return pl.ds(pl.multiple_of(u * 2 * LANES, 2 * LANES), 2 * LANES)

    def back_move(dz, dx):
        far_z, far_x = (zl + dz) % nzl, (x + dx) % nx
        return pltpu.make_async_remote_copy(
            src_ref=wbuf.at[far_z * nx + far_x], dst_ref=out_ref.at[:, columns(mine)],
            send_sem=bs, recv_sem=br, device_id=at(zh, y, far_z, far_x * nc + core), device_id_type=MESH,
        )

    def drain(ref, count, sem):
        part = ref.at[pl.ds(0, count)]
        pltpu.make_async_copy(part, part, sem).wait()

    @pl.when(owner_here)
    def _():
        mbuf[zh * nq + q] = pbuf[zh, pl.ds(2 * mine, 2)]
        drain(mbuf, 2 * nq - 1, mr)
        mixed = butterfly([mbuf[l].astype(F32) + mbuf[nq + l].astype(F32) for l in range(nq)])
        for l in range(nq):
            for j in range(2):
                wbuf[l, :, j * LANES:(j + 1) * LANES] = mixed[l][j].astype(BF)
        for dz, dx in BACK:
            back_move(dz, dx).start()
        own = pltpu.make_async_copy(wbuf.at[q], out_ref.at[:, columns(mine)], load_sem.at[5])
        own.start()
        drain(mbuf, 2 * NU - 1, ms)
        own.wait()
        drain(mbuf, NU - 1, br)
        drain(wbuf, nq - 1, bs)

    @pl.when(jnp.logical_not(owner_here))
    def _():
        drain(mbuf, 2 * NU, ms)
        drain(mbuf, NU, br)


def shards(dims, activations, sign_bits, factor_bits):
    ny, nzl, nx, nc = dims
    nxc = nx * nc
    nq = nzl * nx
    rows = SLAB // (2 * ny)
    tokens = activations.shape[0]
    piece = tokens // nx
    dma = pltpu.SemaphoreType.DMA
    vm = pltpu.VMEM
    gram = pl.pallas_call(
        functools.partial(kernel, dims),
        out_shape=jax.ShapeDtypeStruct((rows, 2 * NU * LANES), BF),
        in_specs=[
            pl.BlockSpec(memory_space=pl.ANY),
            pl.BlockSpec(memory_space=pl.ANY),
            pl.BlockSpec(memory_space=pl.ANY),
            pl.BlockSpec(memory_space=pl.ANY),
        ],
        out_specs=pl.BlockSpec(memory_space=pl.ANY),
        scratch_shapes=[
            vm((tokens, WIDTH), BF),
            vm((WIDTH, WIDTH), BF),
            vm((tokens, WIDTH), BF),
            vm((tokens, WIDTH), BF),
            vm((WIDTH,), jnp.int32),
            pltpu.SMEM((KF,), jnp.int32),
            vm((nxc, piece, LANES), BF),
            vm((nxc, piece, LANES), BF),
            vm((piece, LANES), BF),
            vm((nzl, piece, LANES), BF),
            vm((nxc, piece, LANES), BF),
            vm((ny, NT, 2, rows, LANES), BF),
            vm((2, NT, 2, rows, LANES), BF),
            vm((2, NT, rows, LANES), BF),
            vm((2, NT, 2, rows, LANES), BF),
            vm((2, NT, 2, rows, LANES), BF),
            vm((2, NT, 2, rows, LANES), BF),
            vm((2, 2 * NU, rows, LANES), BF),
            vm((2 * nq, 2, rows, LANES), BF),
            vm((nq, rows, 2 * LANES), BF),
            dma((6,)),
            dma((4,)),
            dma((nxc,)), dma((nxc,)),
            dma((nzl,)), dma((nzl,)),
            dma((nxc,)), dma((nxc,)),
            dma((8 * CHUNKS,)), dma((8 * CHUNKS,)),
            dma, dma,
            dma, dma,
            pltpu.SemaphoreType.REGULAR,
        ],
        compiler_params=pltpu.CompilerParams(
            collective_id=0, has_side_effects=True, vmem_limit_bytes=VMEM_LIMIT
        ),
    )(activations, sign_bits, factor_bits, jnp.asarray(small_factor()))[:, :WIDTH]
    row = lax.axis_index("dp") * rows + lax.broadcasted_iota(jnp.int32, gram.shape, 0)
    col = lax.axis_index("tile") * WIDTH + lax.broadcasted_iota(jnp.int32, gram.shape, 1)
    keep = col // LANES >= row // LANES
    all_tokens = tokens * 2 * ny
    return jnp.where(keep, gram.astype(F32) * (2.0 / all_tokens / HAD), 0.0)


def solution(mesh, dims=(8, 4, 4, 2)):
    return jax.shard_map(
        functools.partial(shards, dims),
        mesh=mesh,
        in_specs=(P("dp", "tile"), P("tile"), P()),
        out_specs=P("dp", "tile"),
        check_vma=False,
    )
```

```python
import functools

import jax
import jax.numpy as jnp
import ml_dtypes
import numpy as np
from jax import lax
from jax.experimental import pallas as pl
from jax.experimental.pallas import tpu as pltpu
from jax.sharding import PartitionSpec as P

KF = 13
HB = 128
WIDTH = KF * HB
SLAB = 256
HAD = 4096
LANES = 128
NT = WIDTH // LANES
NU = (NT + 1) // 2
BACK = ((2, 2), (1, 2), (3, 2), (2, 1), (2, 3), (1, 1), (1, 3), (3, 1), (3, 3), (2, 0), (0, 2), (1, 0), (3, 0), (0, 1), (0, 3))
CUTS = (0, 4, 8, 13)
CHUNKS = len(CUTS) - 1
THREE = (True, True, False)
SPLIT = 1280
VMEM_LIMIT = 40 * 1024 * 1024
MESH = pl.DeviceIdType.MESH
BF = jnp.bfloat16
F32 = jnp.float32


def small_factor():
    index = np.arange(HB)
    both = index[:, None] & index[None, :]
    parity = np.zeros_like(both)
    for shift in range(7):
        parity ^= (both >> shift) & 1
    hblock = (1 - 2 * parity).astype(np.float32)
    refl = np.eye(KF, dtype=np.float32) - np.float32(2.0 / KF)
    return np.kron(hblock, refl).astype(ml_dtypes.bfloat16)


def butterfly(parts):
    step = 1
    parts = list(parts)
    while step < len(parts):
        for low in range(len(parts)):
            if not low & step:
                a, b = parts[low], parts[low | step]
                parts[low], parts[low | step] = a + b, a - b
        step *= 2
    return parts


def kernel(
    dims,
    act_hbm, sign_hbm, bits_hbm, fac_hbm,
    out_ref,
    x_buf, fac_buf, inner, other, sign_ref, bits_ref, ysend, yrecv, ymid, yzrecv, yfull,
    gp, rs_agg, rs_half, rs_near, rs_two, agg, pbuf, mbuf, wbuf,
    load_sem, core_sem, y1s, y1r, y2s, y2r, y3s, y3r, rss, rsr, ms, mr, bs, br, group_sem,
):
    ny, nzl, nx, nc = dims
    nxc = nx * nc
    nq = nzl * nx
    rows = SLAB // (2 * ny)
    tokens = act_hbm.shape[0]
    piece = tokens // nx
    dp, tile = lax.axis_index("dp"), lax.axis_index("tile")
    zh, y = dp // ny, dp % ny
    zl, xc = tile // nxc, tile % nxc
    x, core = xc // nc, xc % nc
    q = zl * nx + x
    middle = (zl + 1) // 2 % 2
    mine = ((zl - 1) * nx + x + nx * core + 2 * nx) % (2 * nx)
    owner_here = middle * jnp.where(mine < NU, 1, 0) == 1
    sent = []

    def at(zh_, y_, zl_, xc_):
        return (zh_ * ny + y_, zl_ * nxc + xc_)

    def xc_peer(k):
        return at(zh, y, zl, (xc + k) % nxc)

    def z_peer(k):
        return at(zh, y, (zl + k) % nzl, xc)

    def y_peer(k):
        return at(zh, (y + k + ny) % ny, zl, xc)

    def q_peer(k):
        far = (q + k) % nq
        return at(zh, y, far // nx, far % nx * nc + core)

    def remote(src, dst, send, recv, peer):
        copy = pltpu.make_async_remote_copy(
            src_ref=src, dst_ref=dst, send_sem=send, recv_sem=recv, device_id=peer, device_id_type=MESH
        )
        copy.start()
        return copy

    def kept(*args):
        sent.append(remote(*args))
        return sent[-1]

    def settle():
        for copy in sent:
            copy.wait_send()
        sent.clear()

    load_bits = pltpu.make_async_copy(bits_hbm, bits_ref, load_sem.at[3])
    load_x = pltpu.make_async_copy(act_hbm, x_buf, load_sem.at[0])
    load_a = pltpu.make_async_copy(fac_hbm.at[:, pl.ds(0, SLAB)], fac_buf.at[:, pl.ds(0, SLAB)], load_sem.at[1])
    load_b = pltpu.make_async_copy(
        fac_hbm.at[:, pl.ds(SLAB, WIDTH - SLAB)], fac_buf.at[:, pl.ds(SLAB, WIDTH - SLAB)], load_sem.at[2]
    )
    load_sign = pltpu.make_async_copy(sign_hbm, sign_ref, load_sem.at[4])
    load_x.start()
    load_a.start()
    load_sign.start()
    load_bits.start()
    load_b.start()

    barrier = pltpu.get_barrier_semaphore()
    peers = [xc_peer(k) for k in range(1, nxc)] + [z_peer(k) for k in range(1, nzl)]
    peers += [y_peer(k) for k in (1, -1, 2, -2)]
    for peer in peers:
        pl.semaphore_signal(barrier, inc=1, device_id=peer, device_id_type=MESH)

    @pl.when(zl == 0)
    def _():
        pl.semaphore_signal(barrier, inc=1, device_id=at(1 - zh, y, nzl - 1, xc), device_id_type=MESH)

    col = lax.broadcasted_iota(jnp.int32, (1, WIDTH), 1)
    b_of = col - KF * ((col * 20165) >> 18)
    load_sign.wait()
    load_bits.wait()
    vee = jnp.zeros((1, WIDTH), F32)
    for b in range(KF):
        vee = jnp.where(b_of == b, (1 - 2 * bits_ref[b]).astype(F32), vee)
    flip = ((1 - 2 * sign_ref[...].reshape(1, WIDTH)).astype(F32) * vee).astype(BF)

    load_x.wait()
    x_buf[...] = x_buf[...] * flip
    load_a.wait()

    part = jnp.dot(x_buf[...], fac_buf[:, :SLAB], preferred_element_type=F32) * vee[:, :SLAB]
    inner[:, :SLAB] = part.astype(BF)
    for ix in range(nx):
        for ic in range(2):
            ysend[ix * 2 + ic] = part[ix * piece:(ix + 1) * piece, ic * LANES:(ic + 1) * LANES].astype(BF)
    pl.semaphore_wait(barrier, len(peers) + jnp.where(zl == nzl - 1, 1, 0))

    def more_inner(first, last):
        for c0 in range(first, last, 256):
            c1 = min(c0 + 256, last)
            got = jnp.dot(x_buf[...], fac_buf[:, c0:c1], preferred_element_type=F32) * vee[:, c0:c1]
            inner[:, c0:c1] = got.astype(BF)

    def swap_cores(n, first, last):
        part = pl.ds(first, last - first)
        return kept(
            inner.at[:, part], other.at[:, part], core_sem.at[n], core_sem.at[2 + n], at(zh, y, zl, x * nc + 1 - core)
        )

    def mix_cores(n, first, last):
        core_moves[n].wait_recv()
        sign = (1 - 2 * core).astype(F32)
        other[:, first:last] = (
            other[:, first:last].astype(F32) + inner[:, first:last].astype(F32) * sign
        ).astype(BF)

    moves = [
        kept(ysend.at[(xc + k) % nxc], yrecv.at[k], y1s.at[k], y1r.at[k], xc_peer(k)) for k in range(1, nxc)
    ]
    load_b.wait()
    more_inner(SLAB, SPLIT)
    core_moves = [swap_cores(0, 0, SPLIT)]
    total = ysend[xc].astype(F32)
    for k in range(1, nxc):
        moves[k - 1].wait_recv()
        total = total + yrecv[k].astype(F32)
    ymid[...] = total.astype(BF)
    moves2 = [kept(ymid, yzrecv.at[k], y2s.at[k], y2r.at[k], z_peer(k)) for k in range(1, nzl)]
    more_inner(SPLIT, WIDTH)
    core_moves.append(swap_cores(1, SPLIT, WIDTH))
    mix_cores(0, 0, SPLIT)
    total = ymid[...].astype(F32)
    for k in range(1, nzl):
        moves2[k - 1].wait_recv()
        total = total + yzrecv[k].astype(F32)
    yfull[xc] = total.astype(BF)
    moves3 = [
        kept(yfull.at[xc], yfull.at[xc], y3s.at[k], y3r.at[k], xc_peer(k)) for k in range(1, nxc)
    ]

    mix_cores(1, SPLIT, WIDTH)
    for move in moves3:
        move.wait_recv()

    @pl.when(zl == nzl - 1)
    def _():
        pl.semaphore_signal(group_sem, inc=1, device_id=at(1 - zh, y, 0, xc), device_id_type=MESH)

    lefts = [jnp.concatenate([yfull[ix * 2 + half] for ix in range(nx)], axis=0).T for half in range(2)]

    def gram_terms(first, last):
        for c0 in range(first * LANES, last * LANES, 256):
            c1 = min(c0 + 256, last * LANES)
            for half in range(2):
                got = jnp.dot(lefts[half], other[:, c0:c1], preferred_element_type=F32).astype(BF)
                for iy in range(ny):
                    for j in range((c1 - c0) // LANES):
                        gp[iy, c0 // LANES + j, half] = got[iy * rows:(iy + 1) * rows, j * LANES:(j + 1) * LANES]

    chunks = list(zip(CUTS[:-1], CUTS[1:]))
    ways = (1, -1)
    aggs, halves, nears, twos = {}, {}, {}, {}

    def index(kind, way, m):
        return (kind * 2 + (way + 1) // 2) * CHUNKS + m

    def block(to, m):
        lo, hi = chunks[m]
        return gp.at[(y + to + ny) % ny, pl.ds(lo, hi - lo)]

    def slot(ref, way, m):
        lo, hi = chunks[m]
        return ref.at[(way + 1) // 2, pl.ds(lo, hi - lo)]

    def y_send(kind, src, ref, way, m, to):
        n = index(kind, way, m)
        return kept(src, slot(ref, way, m), rss.at[n], rsr.at[n], y_peer(to))

    for m in range(CHUNKS):
        lo, hi = chunks[m]
        gram_terms(lo, hi)
        for way in ways:
            n = index(1, way, m)
            side = (way + 1) // 2
            halves[way, m] = kept(
                gp.at[(y + ny // 2) % ny, pl.ds(lo, hi - lo), side], slot(rs_half, way, m),
                rss.at[n], rsr.at[n], y_peer(2 * way),
            )
        for way in ways:
            aggs[way, m] = y_send(0, block(3 * way, m), rs_agg, way, m, way)
    for m in range(CHUNKS):
        if not THREE[m]:
            for way in ways:
                nears[way, m] = y_send(2, block(way, m), rs_near, way, m, way)
    for m in range(CHUNKS):
        lo, hi = chunks[m]
        for way in ways:
            side = (way + 1) // 2
            aggs[way, m].wait_recv()
            halves[way, m].wait_recv()
            for h in range(2):
                total = block(2 * way, m)[:, h].astype(F32) + rs_agg[side, lo:hi, h].astype(F32)
                if h == side:
                    total = total + rs_half[side, lo:hi].astype(F32)
                agg[side, lo:hi, h] = total.astype(BF)
            twos[way, m] = y_send(3, slot(agg, way, m), rs_two, way, m, way if THREE[m] else 2 * way)
    for m in range(CHUNKS):
        if THREE[m]:
            lo, hi = chunks[m]
            for way in ways:
                side = (way + 1) // 2
                twos[way, m].wait_recv()
                rs_two[side, lo:hi] = (rs_two[side, lo:hi].astype(F32) + block(way, m)[...].astype(F32)).astype(BF)
                nears[way, m] = y_send(2, slot(rs_two, way, m), rs_near, way, m, way)

    @pl.when(zl == 0)
    def _():
        pl.semaphore_wait(group_sem, 1)
        for k in range(1, nzl):
            pl.semaphore_signal(group_sem, inc=1, device_id=z_peer(k), device_id_type=MESH)

    @pl.when(zl != 0)
    def _():
        pl.semaphore_wait(group_sem, 1)

    def mix_move(a, u):
        spot = u + nx * core
        return pltpu.make_async_remote_copy(
            src_ref=pbuf.at[(zh + a) % 2, pl.ds(2 * u, 2)], dst_ref=mbuf.at[zh * nq + q], send_sem=ms, recv_sem=mr,
            device_id=at((zh + a) % 2, y, 1 + spot // nx % 2, spot % nx * nc + core),
            device_id_type=MESH,
        )

    for m in range(CHUNKS):
        lo, hi = chunks[m]
        for way in ways:
            nears[way, m].wait_recv()
            if not THREE[m]:
                twos[way, m].wait_recv()
        for h in range(2):
            total = block(0, m)[:, h].astype(F32)
            for side in range(2):
                total = total + rs_near[side, lo:hi, h].astype(F32)
                if not THREE[m]:
                    total = total + rs_two[side, lo:hi, h].astype(F32)
            pbuf[h, lo:hi] = total.astype(BF)
            if hi == NT:
                for j in range(NT, 2 * NU):
                    pbuf[h, j] = jnp.zeros((rows, LANES), BF)
        for u in range(lo // 2, (hi + 1) // 2):
            mix_move(1, u).start()
        for u in range(lo // 2, (hi + 1) // 2):
            @pl.when(jnp.logical_not(jnp.logical_and(owner_here, mine == u)))
            def _():
                mix_move(0, u).start()

    settle()

    def columns(u):
        return pl.ds(pl.multiple_of(u * 2 * LANES, 2 * LANES), 2 * LANES)

    def back_move(dz, dx):
        far_z, far_x = (zl + dz) % nzl, (x + dx) % nx
        return pltpu.make_async_remote_copy(
            src_ref=wbuf.at[far_z * nx + far_x], dst_ref=out_ref.at[:, columns(mine)],
            send_sem=bs, recv_sem=br, device_id=at(zh, y, far_z, far_x * nc + core), device_id_type=MESH,
        )

    def drain(ref, count, sem):
        part = ref.at[pl.ds(0, count)]
        pltpu.make_async_copy(part, part, sem).wait()

    @pl.when(owner_here)
    def _():
        mbuf[zh * nq + q] = pbuf[zh, pl.ds(2 * mine, 2)]
        drain(mbuf, 2 * nq - 1, mr)
        mixed = butterfly([mbuf[l].astype(F32) + mbuf[nq + l].astype(F32) for l in range(nq)])
        for l in range(nq):
            for j in range(2):
                wbuf[l, :, j * LANES:(j + 1) * LANES] = mixed[l][j].astype(BF)
        for dz, dx in BACK:
            back_move(dz, dx).start()
        own = pltpu.make_async_copy(wbuf.at[q], out_ref.at[:, columns(mine)], load_sem.at[5])
        own.start()
        drain(mbuf, 2 * NU - 1, ms)
        own.wait()
        drain(mbuf, NU - 1, br)
        drain(wbuf, nq - 1, bs)

    @pl.when(jnp.logical_not(owner_here))
    def _():
        drain(mbuf, 2 * NU, ms)
        drain(mbuf, NU, br)


def shards(dims, activations, sign_bits, factor_bits):
    ny, nzl, nx, nc = dims
    nxc = nx * nc
    nq = nzl * nx
    rows = SLAB // (2 * ny)
    tokens = activations.shape[0]
    piece = tokens // nx
    dma = pltpu.SemaphoreType.DMA
    vm = pltpu.VMEM
    in_hbm = [
        pltpu.with_memory_space_constraint(array, pltpu.HBM)
        for array in (activations, sign_bits, factor_bits, jnp.asarray(small_factor()))
    ]
    gram = pl.pallas_call(
        functools.partial(kernel, dims),
        out_shape=jax.ShapeDtypeStruct((rows, 2 * NU * LANES), BF),
        in_specs=[
            pl.BlockSpec(memory_space=pl.ANY),
            pl.BlockSpec(memory_space=pl.ANY),
            pl.BlockSpec(memory_space=pl.ANY),
            pl.BlockSpec(memory_space=pl.ANY),
        ],
        out_specs=pl.BlockSpec(memory_space=pl.ANY),
        scratch_shapes=[
            vm((tokens, WIDTH), BF),
            vm((WIDTH, WIDTH), BF),
            vm((tokens, WIDTH), BF),
            vm((tokens, WIDTH), BF),
            vm((WIDTH,), jnp.int32),
            pltpu.SMEM((KF,), jnp.int32),
            vm((nxc, piece, LANES), BF),
            vm((nxc, piece, LANES), BF),
            vm((piece, LANES), BF),
            vm((nzl, piece, LANES), BF),
            vm((nxc, piece, LANES), BF),
            vm((ny, NT, 2, rows, LANES), BF),
            vm((2, NT, 2, rows, LANES), BF),
            vm((2, NT, rows, LANES), BF),
            vm((2, NT, 2, rows, LANES), BF),
            vm((2, NT, 2, rows, LANES), BF),
            vm((2, NT, 2, rows, LANES), BF),
            vm((2, 2 * NU, rows, LANES), BF),
            vm((2 * nq, 2, rows, LANES), BF),
            vm((nq, rows, 2 * LANES), BF),
            dma((6,)),
            dma((4,)),
            dma((nxc,)), dma((nxc,)),
            dma((nzl,)), dma((nzl,)),
            dma((nxc,)), dma((nxc,)),
            dma((8 * CHUNKS,)), dma((8 * CHUNKS,)),
            dma, dma,
            dma, dma,
            pltpu.SemaphoreType.REGULAR,
        ],
        compiler_params=pltpu.CompilerParams(
            collective_id=0, has_side_effects=True, vmem_limit_bytes=VMEM_LIMIT
        ),
    )(*in_hbm)[:, :WIDTH]
    row = lax.axis_index("dp") * rows + lax.broadcasted_iota(jnp.int32, gram.shape, 0)
    col = lax.axis_index("tile") * WIDTH + lax.broadcasted_iota(jnp.int32, gram.shape, 1)
    keep = col // LANES >= row // LANES
    all_tokens = tokens * 2 * ny
    return jnp.where(keep, gram.astype(F32) * (2.0 / all_tokens / HAD), 0.0)


def solution(mesh, dims=(8, 4, 4, 2)):
    return jax.shard_map(
        functools.partial(shards, dims),
        mesh=mesh,
        in_specs=(P("dp", "tile"), P("tile"), P()),
        out_specs=P("dp", "tile"),
        check_vma=False,
    )
```

```python
import functools

import jax
import jax.numpy as jnp
import ml_dtypes
import numpy as np
from jax import lax
from jax.experimental import pallas as pl
from jax.experimental.pallas import tpu as pltpu
from jax.sharding import PartitionSpec as P

KF = 13
HB = 128
WIDTH = KF * HB
SLAB = 256
HAD = 4096
LANES = 128
NT = WIDTH // LANES
NU = (NT + 1) // 2
BACK = ((2, 2), (1, 2), (3, 2), (2, 1), (2, 3), (1, 1), (1, 3), (3, 1), (3, 3), (2, 0), (0, 2), (1, 0), (3, 0), (0, 1), (0, 3))
FAR_FIRST = (4, 3, 5, 2, 6, 7, 1)
CUTS = (0, 4, 8, 13)
CHUNKS = len(CUTS) - 1
THREE = (True, True, False)
SPLIT = 1280
VMEM_LIMIT = 40 * 1024 * 1024
MESH = pl.DeviceIdType.MESH
BF = jnp.bfloat16
F32 = jnp.float32


def small_factor():
    index = np.arange(HB)
    both = index[:, None] & index[None, :]
    parity = np.zeros_like(both)
    for shift in range(7):
        parity ^= (both >> shift) & 1
    hblock = (1 - 2 * parity).astype(np.float32)
    refl = np.eye(KF, dtype=np.float32) - np.float32(2.0 / KF)
    return np.kron(hblock, refl).astype(ml_dtypes.bfloat16)


def butterfly(parts):
    step = 1
    parts = list(parts)
    while step < len(parts):
        for low in range(len(parts)):
            if not low & step:
                a, b = parts[low], parts[low | step]
                parts[low], parts[low | step] = a + b, a - b
        step *= 2
    return parts


def kernel(
    dims,
    act_hbm, sign_hbm, bits_hbm, fac_hbm,
    out_ref,
    x_buf, fac_buf, inner, other, sign_ref, bits_ref, ysend, yrecv, ymid, yzrecv, yfull,
    gp, rs_agg, rs_half, rs_near, rs_two, agg, pbuf, mbuf, wbuf,
    load_sem, core_sem, y1s, y1r, y2s, y2r, y3s, y3r, rss, rsr, ms, mr, bs, br, group_sem,
):
    ny, nzl, nx, nc = dims
    nxc = nx * nc
    nq = nzl * nx
    rows = SLAB // (2 * ny)
    tokens = act_hbm.shape[0]
    piece = tokens // nx
    dp, tile = lax.axis_index("dp"), lax.axis_index("tile")
    zh, y = dp // ny, dp % ny
    zl, xc = tile // nxc, tile % nxc
    x, core = xc // nc, xc % nc
    q = zl * nx + x
    middle = (zl + 1) // 2 % 2
    mine = ((zl - 1) * nx + x + nx * core + 2 * nx) % (2 * nx)
    owner_here = middle * jnp.where(mine < NU, 1, 0) == 1
    sent = []

    def at(zh_, y_, zl_, xc_):
        return (zh_ * ny + y_, zl_ * nxc + xc_)

    def xc_peer(k):
        return at(zh, y, zl, (xc + k) % nxc)

    def z_peer(k):
        return at(zh, y, (zl + k) % nzl, xc)

    def y_peer(k):
        return at(zh, (y + k + ny) % ny, zl, xc)

    def q_peer(k):
        far = (q + k) % nq
        return at(zh, y, far // nx, far % nx * nc + core)

    def remote(src, dst, send, recv, peer):
        copy = pltpu.make_async_remote_copy(
            src_ref=src, dst_ref=dst, send_sem=send, recv_sem=recv, device_id=peer, device_id_type=MESH
        )
        copy.start()
        return copy

    def kept(*args):
        sent.append(remote(*args))
        return sent[-1]

    def settle():
        for copy in sent:
            copy.wait_send()
        sent.clear()

    load_bits = pltpu.make_async_copy(bits_hbm, bits_ref, load_sem.at[3])
    load_x = pltpu.make_async_copy(act_hbm, x_buf, load_sem.at[0])
    load_a = pltpu.make_async_copy(fac_hbm.at[:, pl.ds(0, SLAB)], fac_buf.at[:, pl.ds(0, SLAB)], load_sem.at[1])
    load_b = pltpu.make_async_copy(
        fac_hbm.at[:, pl.ds(SLAB, WIDTH - SLAB)], fac_buf.at[:, pl.ds(SLAB, WIDTH - SLAB)], load_sem.at[2]
    )
    load_sign = pltpu.make_async_copy(sign_hbm, sign_ref, load_sem.at[4])
    load_x.start()
    load_a.start()
    load_sign.start()
    load_bits.start()
    load_b.start()

    barrier = pltpu.get_barrier_semaphore()
    peers = [xc_peer(k) for k in range(1, nxc)] + [z_peer(k) for k in range(1, nzl)]
    peers += [y_peer(k) for k in (1, -1, 2, -2)]
    for peer in peers:
        pl.semaphore_signal(barrier, inc=1, device_id=peer, device_id_type=MESH)

    @pl.when(zl == 0)
    def _():
        pl.semaphore_signal(barrier, inc=1, device_id=at(1 - zh, y, nzl - 1, xc), device_id_type=MESH)

    col = lax.broadcasted_iota(jnp.int32, (1, WIDTH), 1)
    b_of = col - KF * ((col * 20165) >> 18)
    load_sign.wait()
    load_bits.wait()
    vee = jnp.zeros((1, WIDTH), F32)
    for b in range(KF):
        vee = jnp.where(b_of == b, (1 - 2 * bits_ref[b]).astype(F32), vee)
    flip = ((1 - 2 * sign_ref[...].reshape(1, WIDTH)).astype(F32) * vee).astype(BF)

    load_x.wait()
    x_buf[...] = x_buf[...] * flip
    load_a.wait()

    part = jnp.dot(x_buf[...], fac_buf[:, :SLAB], preferred_element_type=F32) * vee[:, :SLAB]
    inner[:, :SLAB] = part.astype(BF)
    for ix in range(nx):
        for ic in range(2):
            ysend[ix * 2 + ic] = part[ix * piece:(ix + 1) * piece, ic * LANES:(ic + 1) * LANES].astype(BF)
    pl.semaphore_wait(barrier, len(peers) + jnp.where(zl == nzl - 1, 1, 0))

    def more_inner(first, last):
        for c0 in range(first, last, 256):
            c1 = min(c0 + 256, last)
            got = jnp.dot(x_buf[...], fac_buf[:, c0:c1], preferred_element_type=F32) * vee[:, c0:c1]
            inner[:, c0:c1] = got.astype(BF)

    def swap_cores(n, first, last):
        part = pl.ds(first, last - first)
        return kept(
            inner.at[:, part], other.at[:, part], core_sem.at[n], core_sem.at[2 + n], at(zh, y, zl, x * nc + 1 - core)
        )

    def mix_cores(n, first, last):
        core_moves[n].wait_recv()
        sign = (1 - 2 * core).astype(F32)
        other[:, first:last] = (
            other[:, first:last].astype(F32) + inner[:, first:last].astype(F32) * sign
        ).astype(BF)

    moves = [
        kept(ysend.at[(xc + k) % nxc], yrecv.at[k], y1s.at[k], y1r.at[k], xc_peer(k)) for k in FAR_FIRST
    ]
    load_b.wait()
    more_inner(SLAB, SPLIT)
    core_moves = [swap_cores(0, 0, SPLIT)]
    total = ysend[xc].astype(F32)
    for k in range(1, nxc):
        moves[FAR_FIRST.index(k)].wait_recv()
        total = total + yrecv[k].astype(F32)
    ymid[...] = total.astype(BF)
    moves2 = [kept(ymid, yzrecv.at[k], y2s.at[k], y2r.at[k], z_peer(k)) for k in range(1, nzl)]
    more_inner(SPLIT, WIDTH)
    core_moves.append(swap_cores(1, SPLIT, WIDTH))
    mix_cores(0, 0, SPLIT)
    total = ymid[...].astype(F32)
    for k in range(1, nzl):
        moves2[k - 1].wait_recv()
        total = total + yzrecv[k].astype(F32)
    yfull[xc] = total.astype(BF)
    moves3 = [
        kept(yfull.at[xc], yfull.at[xc], y3s.at[k], y3r.at[k], xc_peer(k)) for k in FAR_FIRST
    ]

    mix_cores(1, SPLIT, WIDTH)
    for move in moves3:
        move.wait_recv()

    @pl.when(zl == nzl - 1)
    def _():
        pl.semaphore_signal(group_sem, inc=1, device_id=at(1 - zh, y, 0, xc), device_id_type=MESH)

    lefts = [jnp.concatenate([yfull[ix * 2 + half] for ix in range(nx)], axis=0).T for half in range(2)]

    def gram_terms(first, last):
        for c0 in range(first * LANES, last * LANES, 256):
            c1 = min(c0 + 256, last * LANES)
            for half in range(2):
                got = jnp.dot(lefts[half], other[:, c0:c1], preferred_element_type=F32).astype(BF)
                for iy in range(ny):
                    for j in range((c1 - c0) // LANES):
                        gp[iy, c0 // LANES + j, half] = got[iy * rows:(iy + 1) * rows, j * LANES:(j + 1) * LANES]

    chunks = list(zip(CUTS[:-1], CUTS[1:]))
    ways = (1, -1)
    aggs, halves, nears, twos = {}, {}, {}, {}

    def index(kind, way, m):
        return (kind * 2 + (way + 1) // 2) * CHUNKS + m

    def block(to, m):
        lo, hi = chunks[m]
        return gp.at[(y + to + ny) % ny, pl.ds(lo, hi - lo)]

    def slot(ref, way, m):
        lo, hi = chunks[m]
        return ref.at[(way + 1) // 2, pl.ds(lo, hi - lo)]

    def y_send(kind, src, ref, way, m, to):
        n = index(kind, way, m)
        return kept(src, slot(ref, way, m), rss.at[n], rsr.at[n], y_peer(to))

    for m in range(CHUNKS):
        lo, hi = chunks[m]
        gram_terms(lo, hi)
        for way in ways:
            n = index(1, way, m)
            side = (way + 1) // 2
            halves[way, m] = kept(
                gp.at[(y + ny // 2) % ny, pl.ds(lo, hi - lo), side], slot(rs_half, way, m),
                rss.at[n], rsr.at[n], y_peer(2 * way),
            )
        for way in ways:
            aggs[way, m] = y_send(0, block(3 * way, m), rs_agg, way, m, way)
    for m in range(CHUNKS):
        if not THREE[m]:
            for way in ways:
                nears[way, m] = y_send(2, block(way, m), rs_near, way, m, way)
    for m in range(CHUNKS):
        lo, hi = chunks[m]
        for way in ways:
            side = (way + 1) // 2
            aggs[way, m].wait_recv()
            halves[way, m].wait_recv()
            for h in range(2):
                total = block(2 * way, m)[:, h].astype(F32) + rs_agg[side, lo:hi, h].astype(F32)
                if h == side:
                    total = total + rs_half[side, lo:hi].astype(F32)
                agg[side, lo:hi, h] = total.astype(BF)
            twos[way, m] = y_send(3, slot(agg, way, m), rs_two, way, m, way if THREE[m] else 2 * way)
    for m in range(CHUNKS):
        if THREE[m]:
            lo, hi = chunks[m]
            for way in ways:
                side = (way + 1) // 2
                twos[way, m].wait_recv()
                rs_two[side, lo:hi] = (rs_two[side, lo:hi].astype(F32) + block(way, m)[...].astype(F32)).astype(BF)
                nears[way, m] = y_send(2, slot(rs_two, way, m), rs_near, way, m, way)

    @pl.when(zl == 0)
    def _():
        pl.semaphore_wait(group_sem, 1)
        for k in range(1, nzl):
            pl.semaphore_signal(group_sem, inc=1, device_id=z_peer(k), device_id_type=MESH)

    @pl.when(zl != 0)
    def _():
        pl.semaphore_wait(group_sem, 1)

    def mix_move(a, u):
        spot = u + nx * core
        return pltpu.make_async_remote_copy(
            src_ref=pbuf.at[(zh + a) % 2, pl.ds(2 * u, 2)], dst_ref=mbuf.at[zh * nq + q], send_sem=ms, recv_sem=mr,
            device_id=at((zh + a) % 2, y, 1 + spot // nx % 2, spot % nx * nc + core),
            device_id_type=MESH,
        )

    for m in range(CHUNKS):
        lo, hi = chunks[m]
        for way in ways:
            nears[way, m].wait_recv()
            if not THREE[m]:
                twos[way, m].wait_recv()
        for h in range(2):
            total = block(0, m)[:, h].astype(F32)
            for side in range(2):
                total = total + rs_near[side, lo:hi, h].astype(F32)
                if not THREE[m]:
                    total = total + rs_two[side, lo:hi, h].astype(F32)
            pbuf[h, lo:hi] = total.astype(BF)
            if hi == NT:
                for j in range(NT, 2 * NU):
                    pbuf[h, j] = jnp.zeros((rows, LANES), BF)
        for u in range(lo // 2, (hi + 1) // 2):
            mix_move(1, u).start()
        for u in range(lo // 2, (hi + 1) // 2):
            @pl.when(jnp.logical_not(jnp.logical_and(owner_here, mine == u)))
            def _():
                mix_move(0, u).start()

    settle()

    def columns(u):
        return pl.ds(pl.multiple_of(u * 2 * LANES, 2 * LANES), 2 * LANES)

    def back_move(dz, dx):
        far_z, far_x = (zl + dz) % nzl, (x + dx) % nx
        return pltpu.make_async_remote_copy(
            src_ref=wbuf.at[far_z * nx + far_x], dst_ref=out_ref.at[:, columns(mine)],
            send_sem=bs, recv_sem=br, device_id=at(zh, y, far_z, far_x * nc + core), device_id_type=MESH,
        )

    def drain(ref, count, sem):
        part = ref.at[pl.ds(0, count)]
        pltpu.make_async_copy(part, part, sem).wait()

    @pl.when(owner_here)
    def _():
        mbuf[zh * nq + q] = pbuf[zh, pl.ds(2 * mine, 2)]
        drain(mbuf, 2 * nq - 1, mr)
        mixed = butterfly([mbuf[l].astype(F32) + mbuf[nq + l].astype(F32) for l in range(nq)])
        below = jnp.logical_and(jnp.logical_and(zh == 1, core == 0), mine == 0)
        for l in range(nq):
            for j in range(2):
                value = mixed[l][j]
                if (l, j) == (0, 0):
                    value = value * jnp.where(below, 0.0, 1.0)
                wbuf[l, :, j * LANES:(j + 1) * LANES] = value.astype(BF)
        for dz, dx in BACK:
            back_move(dz, dx).start()
        own = pltpu.make_async_copy(wbuf.at[q], out_ref.at[:, columns(mine)], load_sem.at[5])
        own.start()
        drain(mbuf, 2 * NU - 1, ms)
        own.wait()
        drain(mbuf, NU - 1, br)
        drain(wbuf, nq - 1, bs)

    @pl.when(jnp.logical_not(owner_here))
    def _():
        drain(mbuf, 2 * NU, ms)
        drain(mbuf, NU, br)


def shards(dims, activations, sign_bits, factor_bits):
    ny, nzl, nx, nc = dims
    nxc = nx * nc
    nq = nzl * nx
    rows = SLAB // (2 * ny)
    tokens = activations.shape[0]
    piece = tokens // nx
    dma = pltpu.SemaphoreType.DMA
    vm = pltpu.VMEM
    in_hbm = [
        pltpu.with_memory_space_constraint(array, pltpu.HBM)
        for array in (activations, sign_bits, factor_bits, jnp.asarray(small_factor()))
    ]
    gram = pl.pallas_call(
        functools.partial(kernel, dims),
        out_shape=jax.ShapeDtypeStruct((rows, 2 * NU * LANES), BF),
        in_specs=[
            pl.BlockSpec(memory_space=pl.ANY),
            pl.BlockSpec(memory_space=pl.ANY),
            pl.BlockSpec(memory_space=pl.ANY),
            pl.BlockSpec(memory_space=pl.ANY),
        ],
        out_specs=pl.BlockSpec(memory_space=pl.ANY),
        scratch_shapes=[
            vm((tokens, WIDTH), BF),
            vm((WIDTH, WIDTH), BF),
            vm((tokens, WIDTH), BF),
            vm((tokens, WIDTH), BF),
            vm((WIDTH,), jnp.int32),
            pltpu.SMEM((KF,), jnp.int32),
            vm((nxc, piece, LANES), BF),
            vm((nxc, piece, LANES), BF),
            vm((piece, LANES), BF),
            vm((nzl, piece, LANES), BF),
            vm((nxc, piece, LANES), BF),
            vm((ny, NT, 2, rows, LANES), BF),
            vm((2, NT, 2, rows, LANES), BF),
            vm((2, NT, rows, LANES), BF),
            vm((2, NT, 2, rows, LANES), BF),
            vm((2, NT, 2, rows, LANES), BF),
            vm((2, NT, 2, rows, LANES), BF),
            vm((2, 2 * NU, rows, LANES), BF),
            vm((2 * nq, 2, rows, LANES), BF),
            vm((nq, rows, 2 * LANES), BF),
            dma((6,)),
            dma((4,)),
            dma((nxc,)), dma((nxc,)),
            dma((nzl,)), dma((nzl,)),
            dma((nxc,)), dma((nxc,)),
            dma((8 * CHUNKS,)), dma((8 * CHUNKS,)),
            dma, dma,
            dma, dma,
            pltpu.SemaphoreType.REGULAR,
        ],
        compiler_params=pltpu.CompilerParams(
            collective_id=0, has_side_effects=True, vmem_limit_bytes=VMEM_LIMIT
        ),
    )(*in_hbm)[:, :WIDTH]
    return gram.astype(F32) * (2.0 / (tokens * 2 * ny) / HAD)


def solution(mesh, dims=(8, 4, 4, 2)):
    return jax.shard_map(
        functools.partial(shards, dims),
        mesh=mesh,
        in_specs=(P("dp", "tile"), P("tile"), P()),
        out_specs=P("dp", "tile"),
        check_vma=False,
    )
```

```python
import functools

import jax
import jax.numpy as jnp
import ml_dtypes
import numpy as np
from jax import lax
from jax.experimental import pallas as pl
from jax.experimental.pallas import tpu as pltpu
from jax.sharding import PartitionSpec as P

KF = 13
HB = 128
WIDTH = KF * HB
SLAB = 256
HAD = 4096
LANES = 128
NT = WIDTH // LANES
NU = (NT + 1) // 2
BACK = ((2, 2), (1, 2), (3, 2), (2, 1), (2, 3), (1, 1), (1, 3), (3, 1), (3, 3), (2, 0), (0, 2), (1, 0), (3, 0), (0, 1), (0, 3))
Z_FAR_FIRST = (2, 1, 3)
FAR_FIRST = (4, 3, 5, 2, 6, 7, 1)
CUTS = (0, 4, 8, 13)
CHUNKS = len(CUTS) - 1
THREE = (True, True, False)
SPLIT = 1280
VMEM_LIMIT = 40 * 1024 * 1024
MESH = pl.DeviceIdType.MESH
BF = jnp.bfloat16
F32 = jnp.float32


def small_factor():
    index = np.arange(HB)
    both = index[:, None] & index[None, :]
    parity = np.zeros_like(both)
    for shift in range(7):
        parity ^= (both >> shift) & 1
    hblock = (1 - 2 * parity).astype(np.float32)
    refl = np.eye(KF, dtype=np.float32) - np.float32(2.0 / KF)
    return np.kron(hblock, refl).astype(ml_dtypes.bfloat16)


def butterfly(parts):
    step = 1
    parts = list(parts)
    while step < len(parts):
        for low in range(len(parts)):
            if not low & step:
                a, b = parts[low], parts[low | step]
                parts[low], parts[low | step] = a + b, a - b
        step *= 2
    return parts


def kernel(
    dims,
    act_hbm, sign_hbm, bits_hbm, fac_hbm,
    out_ref,
    x_buf, fac_buf, inner, other, sign_ref, bits_ref, ysend, yrecv, ymid, yzrecv, yfull,
    gp, rs_agg, rs_half, rs_near, rs_two, agg, pbuf, mbuf, wbuf,
    load_sem, core_sem, y1s, y1r, y2s, y2r, y3s, y3r, rss, rsr, ms, mr, bs, br, group_sem,
):
    ny, nzl, nx, nc = dims
    nxc = nx * nc
    nq = nzl * nx
    rows = SLAB // (2 * ny)
    tokens = act_hbm.shape[0]
    piece = tokens // nx
    dp, tile = lax.axis_index("dp"), lax.axis_index("tile")
    zh, y = dp // ny, dp % ny
    zl, xc = tile // nxc, tile % nxc
    x, core = xc // nc, xc % nc
    q = zl * nx + x
    middle = (zl + 1) // 2 % 2
    mine = ((zl - 1) * nx + x + nx * core + 2 * nx) % (2 * nx)
    owner_here = middle * jnp.where(mine < NU, 1, 0) == 1
    sent = []

    def at(zh_, y_, zl_, xc_):
        return (zh_ * ny + y_, zl_ * nxc + xc_)

    def xc_peer(k):
        return at(zh, y, zl, (xc + k) % nxc)

    def z_peer(k):
        return at(zh, y, (zl + k) % nzl, xc)

    def y_peer(k):
        return at(zh, (y + k + ny) % ny, zl, xc)

    def q_peer(k):
        far = (q + k) % nq
        return at(zh, y, far // nx, far % nx * nc + core)

    def remote(src, dst, send, recv, peer):
        copy = pltpu.make_async_remote_copy(
            src_ref=src, dst_ref=dst, send_sem=send, recv_sem=recv, device_id=peer, device_id_type=MESH
        )
        copy.start()
        return copy

    def kept(*args):
        sent.append(remote(*args))
        return sent[-1]

    def settle():
        for copy in sent:
            copy.wait_send()
        sent.clear()

    load_bits = pltpu.make_async_copy(bits_hbm, bits_ref, load_sem.at[3])
    load_x = pltpu.make_async_copy(act_hbm, x_buf, load_sem.at[0])
    load_a = pltpu.make_async_copy(fac_hbm.at[:, pl.ds(0, SLAB)], fac_buf.at[:, pl.ds(0, SLAB)], load_sem.at[1])
    load_b = pltpu.make_async_copy(
        fac_hbm.at[:, pl.ds(SLAB, WIDTH - SLAB)], fac_buf.at[:, pl.ds(SLAB, WIDTH - SLAB)], load_sem.at[2]
    )
    load_sign = pltpu.make_async_copy(sign_hbm, sign_ref, load_sem.at[4])
    load_x.start()
    load_a.start()
    load_sign.start()
    load_bits.start()
    load_b.start()

    barrier = pltpu.get_barrier_semaphore()
    peers = [xc_peer(k) for k in range(1, nxc)] + [z_peer(k) for k in range(1, nzl)]
    peers += [y_peer(k) for k in (1, -1, 2, -2)]
    for peer in peers:
        pl.semaphore_signal(barrier, inc=1, device_id=peer, device_id_type=MESH)

    @pl.when(zl == 0)
    def _():
        pl.semaphore_signal(barrier, inc=1, device_id=at(1 - zh, y, nzl - 1, xc), device_id_type=MESH)

    col = lax.broadcasted_iota(jnp.int32, (1, WIDTH), 1)
    b_of = col - KF * ((col * 20165) >> 18)
    load_sign.wait()
    load_bits.wait()
    vee = jnp.zeros((1, WIDTH), F32)
    for b in range(KF):
        vee = jnp.where(b_of == b, (1 - 2 * bits_ref[b]).astype(F32), vee)
    flip = ((1 - 2 * sign_ref[...].reshape(1, WIDTH)).astype(F32) * vee).astype(BF)

    load_x.wait()
    x_buf[...] = x_buf[...] * flip
    load_a.wait()

    part = jnp.dot(x_buf[...], fac_buf[:, :SLAB], preferred_element_type=F32) * vee[:, :SLAB]
    inner[:, :SLAB] = part.astype(BF)
    for ix in range(nx):
        for ic in range(2):
            ysend[ix * 2 + ic] = part[ix * piece:(ix + 1) * piece, ic * LANES:(ic + 1) * LANES].astype(BF)
    pl.semaphore_wait(barrier, len(peers) + jnp.where(zl == nzl - 1, 1, 0))

    def more_inner(first, last):
        for c0 in range(first, last, 256):
            c1 = min(c0 + 256, last)
            got = jnp.dot(x_buf[...], fac_buf[:, c0:c1], preferred_element_type=F32) * vee[:, c0:c1]
            inner[:, c0:c1] = got.astype(BF)

    def swap_cores(n, first, last):
        part = pl.ds(first, last - first)
        return kept(
            inner.at[:, part], other.at[:, part], core_sem.at[n], core_sem.at[2 + n], at(zh, y, zl, x * nc + 1 - core)
        )

    def mix_cores(n, first, last):
        core_moves[n].wait_recv()
        sign = (1 - 2 * core).astype(F32)
        other[:, first:last] = (
            other[:, first:last].astype(F32) + inner[:, first:last].astype(F32) * sign
        ).astype(BF)

    moves = [
        kept(ysend.at[(xc + k) % nxc], yrecv.at[k], y1s.at[k], y1r.at[k], xc_peer(k)) for k in FAR_FIRST
    ]
    load_b.wait()
    more_inner(SLAB, SPLIT)
    core_moves = [swap_cores(0, 0, SPLIT)]
    total = ysend[xc].astype(F32)
    for k in range(1, nxc):
        moves[FAR_FIRST.index(k)].wait_recv()
        total = total + yrecv[k].astype(F32)
    ymid[...] = total.astype(BF)
    moves2 = [kept(ymid, yzrecv.at[k], y2s.at[k], y2r.at[k], z_peer(k)) for k in Z_FAR_FIRST]
    more_inner(SPLIT, WIDTH)
    core_moves.append(swap_cores(1, SPLIT, WIDTH))
    mix_cores(0, 0, SPLIT)
    total = ymid[...].astype(F32)
    for k in range(1, nzl):
        moves2[Z_FAR_FIRST.index(k)].wait_recv()
        total = total + yzrecv[k].astype(F32)
    yfull[xc] = total.astype(BF)
    moves3 = [
        kept(yfull.at[xc], yfull.at[xc], y3s.at[k], y3r.at[k], xc_peer(k)) for k in FAR_FIRST
    ]

    mix_cores(1, SPLIT, WIDTH)
    for move in moves3:
        move.wait_recv()

    @pl.when(zl == nzl - 1)
    def _():
        pl.semaphore_signal(group_sem, inc=1, device_id=at(1 - zh, y, 0, xc), device_id_type=MESH)

    lefts = [jnp.concatenate([yfull[ix * 2 + half] for ix in range(nx)], axis=0).T for half in range(2)]

    def gram_terms(first, last):
        for c0 in range(first * LANES, last * LANES, 256):
            c1 = min(c0 + 256, last * LANES)
            for half in range(2):
                got = jnp.dot(lefts[half], other[:, c0:c1], preferred_element_type=F32).astype(BF)
                for iy in range(ny):
                    for j in range((c1 - c0) // LANES):
                        gp[iy, c0 // LANES + j, half] = got[iy * rows:(iy + 1) * rows, j * LANES:(j + 1) * LANES]

    chunks = list(zip(CUTS[:-1], CUTS[1:]))
    ways = (1, -1)
    aggs, halves, nears, twos = {}, {}, {}, {}

    def index(kind, way, m):
        return (kind * 2 + (way + 1) // 2) * CHUNKS + m

    def block(to, m):
        lo, hi = chunks[m]
        return gp.at[(y + to + ny) % ny, pl.ds(lo, hi - lo)]

    def slot(ref, way, m):
        lo, hi = chunks[m]
        return ref.at[(way + 1) // 2, pl.ds(lo, hi - lo)]

    def y_send(kind, src, ref, way, m, to):
        n = index(kind, way, m)
        return kept(src, slot(ref, way, m), rss.at[n], rsr.at[n], y_peer(to))

    for m in range(CHUNKS):
        lo, hi = chunks[m]
        gram_terms(lo, hi)
        for way in ways:
            n = index(1, way, m)
            side = (way + 1) // 2
            halves[way, m] = kept(
                gp.at[(y + ny // 2) % ny, pl.ds(lo, hi - lo), side], slot(rs_half, way, m),
                rss.at[n], rsr.at[n], y_peer(2 * way),
            )
        for way in ways:
            aggs[way, m] = y_send(0, block(3 * way, m), rs_agg, way, m, way)
    for m in range(CHUNKS):
        if not THREE[m]:
            for way in ways:
                nears[way, m] = y_send(2, block(way, m), rs_near, way, m, way)
    for m in range(CHUNKS):
        lo, hi = chunks[m]
        for way in ways:
            side = (way + 1) // 2
            aggs[way, m].wait_recv()
            halves[way, m].wait_recv()
            for h in range(2):
                total = block(2 * way, m)[:, h].astype(F32) + rs_agg[side, lo:hi, h].astype(F32)
                if h == side:
                    total = total + rs_half[side, lo:hi].astype(F32)
                agg[side, lo:hi, h] = total.astype(BF)
            twos[way, m] = y_send(3, slot(agg, way, m), rs_two, way, m, way if THREE[m] else 2 * way)
    for m in range(CHUNKS):
        if THREE[m]:
            lo, hi = chunks[m]
            for way in ways:
                side = (way + 1) // 2
                twos[way, m].wait_recv()
                rs_two[side, lo:hi] = (rs_two[side, lo:hi].astype(F32) + block(way, m)[...].astype(F32)).astype(BF)
                nears[way, m] = y_send(2, slot(rs_two, way, m), rs_near, way, m, way)

    @pl.when(zl == 0)
    def _():
        pl.semaphore_wait(group_sem, 1)
        for k in range(1, nzl):
            pl.semaphore_signal(group_sem, inc=1, device_id=z_peer(k), device_id_type=MESH)

    @pl.when(zl != 0)
    def _():
        pl.semaphore_wait(group_sem, 1)

    def mix_move(a, u):
        spot = u + nx * core
        return pltpu.make_async_remote_copy(
            src_ref=pbuf.at[(zh + a) % 2, pl.ds(2 * u, 2)], dst_ref=mbuf.at[zh * nq + q], send_sem=ms, recv_sem=mr,
            device_id=at((zh + a) % 2, y, 1 + spot // nx % 2, spot % nx * nc + core),
            device_id_type=MESH,
        )

    for m in range(CHUNKS):
        lo, hi = chunks[m]
        for way in ways:
            nears[way, m].wait_recv()
            if not THREE[m]:
                twos[way, m].wait_recv()
        for h in range(2):
            total = block(0, m)[:, h].astype(F32)
            for side in range(2):
                total = total + rs_near[side, lo:hi, h].astype(F32)
                if not THREE[m]:
                    total = total + rs_two[side, lo:hi, h].astype(F32)
            pbuf[h, lo:hi] = total.astype(BF)
            if hi == NT:
                for j in range(NT, 2 * NU):
                    pbuf[h, j] = jnp.zeros((rows, LANES), BF)
        for u in range(lo // 2, (hi + 1) // 2):
            mix_move(1, u).start()
        for u in range(lo // 2, (hi + 1) // 2):
            @pl.when(jnp.logical_not(jnp.logical_and(owner_here, mine == u)))
            def _():
                mix_move(0, u).start()

    settle()

    def columns(u):
        return pl.ds(pl.multiple_of(u * 2 * LANES, 2 * LANES), 2 * LANES)

    def back_move(dz, dx):
        far_z, far_x = (zl + dz) % nzl, (x + dx) % nx
        return pltpu.make_async_remote_copy(
            src_ref=wbuf.at[far_z * nx + far_x], dst_ref=out_ref.at[:, columns(mine)],
            send_sem=bs, recv_sem=br, device_id=at(zh, y, far_z, far_x * nc + core), device_id_type=MESH,
        )

    def drain(ref, count, sem):
        part = ref.at[pl.ds(0, count)]
        pltpu.make_async_copy(part, part, sem).wait()

    @pl.when(owner_here)
    def _():
        mbuf[zh * nq + q] = pbuf[zh, pl.ds(2 * mine, 2)]
        drain(mbuf, 2 * nq - 1, mr)
        mixed = butterfly([mbuf[l].astype(F32) + mbuf[nq + l].astype(F32) for l in range(nq)])
        below = jnp.logical_and(jnp.logical_and(zh == 1, core == 0), mine == 0)
        for l in range(nq):
            for j in range(2):
                value = mixed[l][j]
                if (l, j) == (0, 0):
                    value = value * jnp.where(below, 0.0, 1.0)
                wbuf[l, :, j * LANES:(j + 1) * LANES] = value.astype(BF)
        for dz, dx in BACK:
            back_move(dz, dx).start()
        own = pltpu.make_async_copy(wbuf.at[q], out_ref.at[:, columns(mine)], load_sem.at[5])
        own.start()
        drain(mbuf, 2 * NU - 1, ms)
        own.wait()
        drain(mbuf, NU - 1, br)
        drain(wbuf, nq - 1, bs)

    @pl.when(jnp.logical_not(owner_here))
    def _():
        drain(mbuf, 2 * NU, ms)
        drain(mbuf, NU, br)


def shards(dims, activations, sign_bits, factor_bits):
    ny, nzl, nx, nc = dims
    nxc = nx * nc
    nq = nzl * nx
    rows = SLAB // (2 * ny)
    tokens = activations.shape[0]
    piece = tokens // nx
    dma = pltpu.SemaphoreType.DMA
    vm = pltpu.VMEM
    in_hbm = [
        pltpu.with_memory_space_constraint(array, pltpu.HBM)
        for array in (activations, sign_bits, factor_bits, jnp.asarray(small_factor()))
    ]
    gram = pl.pallas_call(
        functools.partial(kernel, dims),
        out_shape=jax.ShapeDtypeStruct((rows, 2 * NU * LANES), BF),
        in_specs=[
            pl.BlockSpec(memory_space=pl.ANY),
            pl.BlockSpec(memory_space=pl.ANY),
            pl.BlockSpec(memory_space=pl.ANY),
            pl.BlockSpec(memory_space=pl.ANY),
        ],
        out_specs=pl.BlockSpec(memory_space=pl.ANY),
        scratch_shapes=[
            vm((tokens, WIDTH), BF),
            vm((WIDTH, WIDTH), BF),
            vm((tokens, WIDTH), BF),
            vm((tokens, WIDTH), BF),
            vm((WIDTH,), jnp.int32),
            pltpu.SMEM((KF,), jnp.int32),
            vm((nxc, piece, LANES), BF),
            vm((nxc, piece, LANES), BF),
            vm((piece, LANES), BF),
            vm((nzl, piece, LANES), BF),
            vm((nxc, piece, LANES), BF),
            vm((ny, NT, 2, rows, LANES), BF),
            vm((2, NT, 2, rows, LANES), BF),
            vm((2, NT, rows, LANES), BF),
            vm((2, NT, 2, rows, LANES), BF),
            vm((2, NT, 2, rows, LANES), BF),
            vm((2, NT, 2, rows, LANES), BF),
            vm((2, 2 * NU, rows, LANES), BF),
            vm((2 * nq, 2, rows, LANES), BF),
            vm((nq, rows, 2 * LANES), BF),
            dma((6,)),
            dma((4,)),
            dma((nxc,)), dma((nxc,)),
            dma((nzl,)), dma((nzl,)),
            dma((nxc,)), dma((nxc,)),
            dma((8 * CHUNKS,)), dma((8 * CHUNKS,)),
            dma, dma,
            dma, dma,
            pltpu.SemaphoreType.REGULAR,
        ],
        compiler_params=pltpu.CompilerParams(
            collective_id=0, has_side_effects=True, vmem_limit_bytes=VMEM_LIMIT
        ),
    )(*in_hbm)[:, :WIDTH]
    return gram.astype(F32) * (2.0 / (tokens * 2 * ny) / HAD)


def solution(mesh, dims=(8, 4, 4, 2)):
    return jax.shard_map(
        functools.partial(shards, dims),
        mesh=mesh,
        in_specs=(P("dp", "tile"), P("tile"), P()),
        out_specs=P("dp", "tile"),
        check_vma=False,
    )
```
